256 devices in a mesh: tower: 2 (over core), dp: 64 (over y, x_hi, z), mp: 2 (over x_lo).
Axes of the slice: x: 4 (x_hi: 2, x_lo: 2; x = x_hi * 2 + x_lo), y: 4, z: 8, core: 2. Of those that a mesh axis runs over, the one named last changes fastest.
Arguments:
- image_feats: bfloat16 [65536, 1024], P('dp'), may hold values from -6 to 6
- text_feats: bfloat16 [65536, 768], P('dp'), may hold values from -6 to 6
- image_gain: float32 [1024], replicated, may hold values from 0.1 to 1.9
- image_bias: float32 [1024], replicated, may hold values from -4 to 4
- text_gain: float32 [768], replicated, may hold values from 0.1 to 1.9
- text_bias: float32 [768], replicated, may hold values from -4 to 4
- image_head: bfloat16 [1024, 1024], P(None, 'mp'), may hold values from -0.1875 to 0.1875
- text_head: bfloat16 [768, 1024], P(None, 'mp'), may hold values from -0.21875 to 0.21875
- running_cov: float32 [2, 1024, 1024], P('tower'), as said below
- pair_index: int32 [65536], P('dp'), may hold values from 0 to 65535, as said below
Outputs:
- new_cov: float32 [2, 1024, 1024], P('tower', None, 'mp')
- head_grads: float32 [1792, 1024], P(('tower', 'dp'), 'mp')
- norm_grads: float32 [2, 1792], replicated
- loss: float32 [2], replicated
The draws below stay inside these ranges and needn't reach their ends.
Inputs may be any that keep to these rules, and one draw needn't show every extreme that they name: `pair_index`: each aligned block of 1024 entries (the rows of one index of dp) is a permutation of that block's own row numbers. `running_cov`: both matrices are symmetric and positive definite.
All inputs are finite; a program needn't handle non-finite values.
Results may differ from the reference program's by a relative error of at most 0.0003.
Values may be sent and summed in bfloat16 or wider, within the bound.
No kernel may reach another device: no remote copies, remote signals or barrier semaphores. Data moves between devices by JAX's collectives and lax.ppermute only.
A program may use at most 128 MiB of HBM per device.

```python
import math
import jax
import jax.numpy as jnp
from jax import lax

IMG_W = 1024
TXT_W = 768
HEAD = 1024
ROWS = 1024
PAIRS = 65536


def draw_running_cov(key, part):
    key = jax.random.fold_in(key, 11)
    first, second, third = jax.random.split(key, 3)
    raw = jax.random.uniform(first, (2, HEAD, HEAD), jnp.float32, -1.0, 1.0)
    symmetric = 0.5 * (raw + jnp.swapaxes(raw, 1, 2))
    positions = jnp.arange(HEAD)
    identity = (positions[:, None] == positions[None, :]).astype(jnp.float32)
    diagonal = 1.0 + 0.5 * jax.random.uniform(second, (2, HEAD), jnp.float32)
    low_end, high_end = (0.4, 4.0)
    scales = jnp.exp(jax.random.uniform(third, (2, HEAD), jnp.float32, math.log(low_end), math.log(high_end)))
    inner = symmetric * (0.9 / HEAD) * (1.0 - identity) + identity[None] * diagonal[:, :, None]
    return (scales[:, :, None] * inner * scales[:, None, :]).astype(jnp.float32)


def draw_pair_index(key, part):
    key = jax.random.fold_in(key, 7)
    blocks = PAIRS // ROWS
    keys = jax.random.split(key, blocks)
    perms = jax.vmap(lambda single: jax.random.permutation(single, ROWS))(keys)
    offsets = jnp.arange(blocks, dtype=jnp.int32)[:, None] * ROWS
    return (perms.astype(jnp.int32) + offsets).reshape(PAIRS).astype(jnp.int32)


def level_of(stream_key, shape, cuts, low, top_value):
    factor_of = 1.0
    for dim, blocks in cuts:
        draws = jax.random.uniform(jax.random.fold_in(jax.random.fold_in(stream_key, 6), dim), (blocks,), jnp.float32, low / len(cuts), top_value / len(cuts))
        factor_of = factor_of * jnp.repeat(jnp.exp(draws), shape[dim] // blocks).reshape((-1,) + (1,) * (len(shape) - 1 - dim))
    return factor_of


def normal_values(own_key, dims, spread, limit, pieces=(), kind=jnp.bfloat16):
    entries = jax.random.normal(own_key, dims, jnp.float32) * spread
    if len(pieces) > 0:
        entries = level_of(own_key, dims, pieces, -0.22, 0.18) * entries
    return jnp.clip(entries, min=-limit, max=limit).astype(kind)


def setup_inputs(seed: int = 0) -> dict:
    seeds = jax.random.split(jax.random.key(seed), 11)
    return {
        "image_feats": normal_values(seeds[0], (PAIRS, IMG_W), 1.0, 6.0, ((0, 64),)),
        "text_feats": normal_values(seeds[1], (PAIRS, TXT_W), 1.0, 6.0, ((0, 64),)),
        "image_gain": jnp.clip(1.0 + 0.18 * jax.random.normal(seeds[2], (IMG_W,), jnp.float32), 0.1, 1.9),
        "image_bias": normal_values(seeds[3], (IMG_W,), 1.0, 4.0, (), jnp.float32),
        "text_gain": jnp.clip(1.0 + 0.18 * jax.random.normal(seeds[4], (TXT_W,), jnp.float32), 0.1, 1.9),
        "text_bias": normal_values(seeds[5], (TXT_W,), 1.0, 4.0, (), jnp.float32),
        "image_head": normal_values(seeds[6], (IMG_W, HEAD), IMG_W ** -0.5, 0.1875, ((1, 2),)),
        "text_head": normal_values(seeds[7], (TXT_W, HEAD), TXT_W ** -0.5, 0.21875, ((1, 2),)),
        "running_cov": draw_running_cov(jax.random.fold_in(seeds[10], 71), 0),
        "pair_index": draw_pair_index(jax.random.fold_in(seeds[10], 71), 0),
    }


epsilon = 1e-05

def normalize(features, gain_vec, shift_vec):
    values = features.astype(jnp.float32)
    row_mean = lax.optimization_barrier(jnp.mean(values, axis=1, keepdims=True))
    centered = values - row_mean
    row_var = lax.optimization_barrier(jnp.mean(centered * centered, axis=1, keepdims=True))
    standard = centered * lax.rsqrt(row_var + epsilon)
    normed = (standard * gain_vec[None, :] + shift_vec[None, :]).astype(jnp.bfloat16)
    return (standard, normed)

def whiten(projected_low, cov_old):
    product = jnp.dot(projected_low.T.astype(jnp.float32), projected_low.astype(jnp.float32), preferred_element_type=jnp.float32)
    cov_new = 0.5 * cov_old + 0.5 * product / PAIRS
    factor = jnp.linalg.cholesky(cov_new)
    inverse = lax.linalg.triangular_solve(factor, jnp.eye(HEAD, dtype=jnp.float32), left_side=True, lower=True)
    whitened = jnp.dot(projected_low.astype(jnp.float32), inverse.T, precision=lax.Precision.HIGHEST)
    return (cov_new, whitened.astype(jnp.bfloat16))

def backward(standard, normed, grad_low, weights):
    weight_grad = jnp.dot(normed.T.astype(jnp.float32), grad_low.astype(jnp.float32), preferred_element_type=jnp.float32)
    dnormed = jnp.dot(grad_low.astype(jnp.float32), weights.T.astype(jnp.float32), preferred_element_type=jnp.float32)
    return (weight_grad, lax.optimization_barrier(jnp.sum(standard * dnormed, axis=0)), lax.optimization_barrier(jnp.sum(dnormed, axis=0)))

def reference(image_feats, text_feats, image_gain, image_bias, text_gain, text_bias, image_head, text_head, running_cov, pair_index):
    image_std, image_normed = normalize(image_feats, image_gain, image_bias)
    text_std, text_normed = normalize(text_feats, text_gain, text_bias)
    image_proj = jnp.dot(image_normed.astype(jnp.float32), image_head.astype(jnp.float32), preferred_element_type=jnp.float32)
    text_proj = jnp.dot(text_normed.astype(jnp.float32), text_head.astype(jnp.float32), preferred_element_type=jnp.float32)
    image_cov, image_white = whiten(image_proj.astype(jnp.bfloat16), running_cov[0])
    text_cov, text_white = whiten(text_proj.astype(jnp.bfloat16), running_cov[1])
    inverse_pairs = jnp.zeros((PAIRS,), jnp.int32).at[pair_index].set(jnp.arange(PAIRS, dtype=jnp.int32))
    image_target = text_white[pair_index].astype(jnp.float32)
    text_target = image_white[inverse_pairs].astype(jnp.float32)
    image_resid = image_proj - image_target
    text_resid = text_proj - text_target
    scale = 1.0 / (2.0 * PAIRS * HEAD)
    loss = jnp.stack([jnp.sum(image_resid * image_resid) * scale, jnp.sum(text_resid * text_resid) * scale])
    image_grad = (image_resid / HEAD).astype(jnp.bfloat16)
    text_grad = (text_resid / HEAD).astype(jnp.bfloat16)
    image_w, image_g, image_b = backward(image_std, image_normed, image_grad, image_head)
    text_w, text_g, text_b = backward(text_std, text_normed, text_grad, text_head)
    new_cov = jnp.stack([image_cov, text_cov])
    head_grads = jnp.concatenate([image_w, text_w], axis=0)
    norm_grads = jnp.stack([jnp.concatenate([image_g, text_g]), jnp.concatenate([image_b, text_b])])
    return (new_cov, head_grads, norm_grads, loss)
```

```python
import jax
import jax.numpy as jnp
from jax import lax
from jax.experimental import pallas as pl
from jax.experimental.pallas import tpu as pltpu
from jax.sharding import PartitionSpec as P

EPSILON = 1e-05
F32 = jnp.float32
BF16 = jnp.bfloat16
BLOCK = 128
GROUP = 8
PANELS = {
    1: ((0, 0, 8), (1, 0, 8), (2, 2, 2), (3, 2, 2)),
    0: ((2, 4, 4), (3, 4, 4), (4, 4, 4), (5, 4, 4), (6, 6, 2), (7, 6, 2)),
}
PANEL_ROWS = 20 * BLOCK


def flip(value, axis):
    return lax.ppermute(value, axis, [(0, 1), (1, 0)])


def swap_halves(value):
    dp_count = lax.axis_size("dp")
    x_hi_bit = 8 if dp_count == 64 else 1
    pairs = []
    for dp in range(dp_count):
        for mp in range(2):
            x_hi = (dp // x_hi_bit) % 2
            x = (x_hi * 2 + mp + (-1 if mp == 0 else 1)) % 4
            other = dp - x_hi * x_hi_bit + (x // 2) * x_hi_bit
            pairs.append((dp * 2 + mp, other * 2 + x % 2))
    half = value.shape[0] // 2
    near = flip(value[:half], "mp")
    far = lax.ppermute(value[half:], ("dp", "mp"), pairs)
    return near, far


def normalize(features, gain, bias):
    values = features.astype(F32)
    mean = jnp.mean(values, axis=1, keepdims=True)
    centered = values - mean
    var = jnp.mean(centered * centered, axis=1, keepdims=True)
    standard = centered * lax.rsqrt(var + EPSILON)
    return standard, (standard * gain[None, :] + bias[None, :]).astype(BF16)


def pad_cols(value, width):
    return jnp.pad(value, ((0, 0), (0, width - value.shape[1])))


def pad_rows(value, height):
    return jnp.pad(value, ((0, height - value.shape[0]), (0, 0)))


def contract_rows(a, b):
    return lax.dot_general(a, b, (((0,), (0,)), ((), ())), preferred_element_type=F32)


def precise_dot(a, b, dims):
    return lax.dot_general(
        a, b, (dims, ((), ())), precision=lax.Precision.HIGHEST, preferred_element_type=F32
    )


def factor_block(w_ref, t_ref):
    n = w_ref.shape[0]
    sub = lax.broadcasted_iota(jnp.int32, (GROUP, n), 0)
    lane = lax.broadcasted_iota(jnp.int32, (GROUP, n), 1)
    rows = [w_ref[GROUP * i : GROUP * (i + 1), :] for i in range(n // GROUP)]

    def spread(value):
        return jnp.broadcast_to(value, (GROUP, n))

    for g in range(n // GROUP):
        first = GROUP * g
        current = rows[g]
        inside = (lane >= first) & (lane < first + GROUP)
        cols = [spread(current[:, first + j : first + j + 1]) for j in range(GROUP)]
        full = jnp.where(inside, jnp.where(lane - first == sub, 1.0, 0.0), current)
        result = jnp.zeros((GROUP, n), F32)
        for j in range(GROUP):
            root = lax.rsqrt(spread(cols[j][j : j + 1, :]))
            recip = root * root
            here = sub == j
            row = spread(full[j : j + 1, :])
            result = jnp.where(here, row * root, result)
            scaled = row * recip
            full = jnp.where(here, scaled, full - cols[j] * scaled)
            for k in range(j + 1, GROUP):
                factor = spread(cols[k][j : j + 1, :]) * recip
                cols[k] = jnp.where(here, factor, cols[k] - cols[j] * factor)
        t_ref[first : first + GROUP, :] = jnp.where(lane < first + GROUP, result, 0.0)
        spreads = [spread(full[k : k + 1, :]) for k in range(GROUP)]
        for i in range(g + 1, n // GROUP):
            value = rows[i]
            terms = [
                spread(value[:, first + k : first + k + 1]) * spreads[k] for k in range(GROUP)
            ]
            while len(terms) > 1:
                terms = [terms[a] + terms[a + 1] for a in range(0, len(terms), 2)]
            rows[i] = jnp.where(inside, 0.0, value) - terms[0]


def whitening_kernel(total_rows, mp_ref, lo_ref, hi_ref, old_ref, inv_ref, cov_ref, w, blk, t, y):
    n = old_ref.shape[0]
    blocks = n // BLOCK
    scale = 0.5 / total_rows
    for source, panels in ((lo_ref, PANELS[1]), (hi_ref, PANELS[0])):
        offset = 0
        for col, row, count in panels:
            for i in range(row, row + count):
                here = slice(i * BLOCK, (i + 1) * BLOCK)
                there = slice(col * BLOCK, (col + 1) * BLOCK)
                value = (
                    0.5 * old_ref[here, there] + scale * source[offset : offset + BLOCK, :]
                )
                w[here, there] = value
                if i // 2 > col // 2:
                    w[there, here] = value.T
                offset += BLOCK
    half = cov_ref.shape[1]
    cov_ref[...] = w[:, pl.ds(pl.multiple_of(mp_ref[0] * half, half), half)]
    lane = lax.broadcasted_iota(jnp.int32, (BLOCK, n), 1)
    sub = lax.broadcasted_iota(jnp.int32, (BLOCK, n), 0)

    def step(k, carry):
        r = pl.ds(pl.multiple_of(k * BLOCK, BLOCK), BLOCK)
        blk[...] = w[r, r]
        factor_block(blk, t)
        inside = (lane >= k * BLOCK) & (lane < k * BLOCK + BLOCK)
        current = jnp.where(inside, jnp.where(lane - k * BLOCK == sub, 1.0, 0.0), w[r, :])
        small = t[...]
        result = precise_dot(small, current, ((1,), (0,)))
        inv_ref[r, :] = jnp.where(lane < (k + 1) * BLOCK, result, 0.0)
        y[...] = precise_dot(small, result, ((0,), (0,)))

        def update(i, carry):
            q = pl.ds(pl.multiple_of(i * BLOCK, BLOCK), BLOCK)
            left = w[q, r]
            w[q, :] = jnp.where(inside, 0.0, w[q, :]) - precise_dot(left, y[...], ((1,), (0,)))
            return carry

        lax.fori_loop(k + 1, blocks, update, 0)
        return carry

    lax.fori_loop(0, blocks, step, 0)


def inverse_factor(mp_index, lo, hi, cov_old, total_rows):
    n = cov_old.shape[0]
    vmem = pl.BlockSpec(memory_space=pltpu.VMEM)

    def kernel(*refs):
        whitening_kernel(total_rows, *refs)

    return pl.pallas_call(
        kernel,
        out_shape=(
            jax.ShapeDtypeStruct((n, n), F32),
            jax.ShapeDtypeStruct((n, n // 2), F32),
        ),
        in_specs=[pl.BlockSpec(memory_space=pltpu.SMEM), vmem, vmem, vmem],
        out_specs=(vmem, vmem),
        scratch_shapes=[
            pltpu.VMEM((n, n), F32),
            pltpu.VMEM((BLOCK, BLOCK), F32),
            pltpu.VMEM((BLOCK, BLOCK), F32),
            pltpu.VMEM((BLOCK, n), F32),
        ],
        compiler_params=pltpu.CompilerParams(vmem_limit_bytes=48 * 1024 * 1024),
        cost_estimate=pl.CostEstimate(flops=6 * 10**9, bytes_accessed=10**7, transcendentals=0),
        name="inverse_factor",
    )(mp_index, lo, hi, cov_old)


def fixed_scale(exponent):
    return jnp.exp2(exponent - 15.0)


def to_fixed(value, axis):
    top = jnp.maximum(jnp.max(jnp.abs(value), axis=axis, keepdims=True), 1e-30)
    exponent = jnp.ceil(jnp.log2(top))
    codes = jnp.clip(jnp.round(value / fixed_scale(exponent)), -32767.0, 32767.0)
    return codes.astype(jnp.int16), exponent.astype(jnp.int16)


def from_fixed(codes, exponent):
    return codes.astype(F32) * fixed_scale(exponent.astype(F32))


def body(
    image_feats,
    text_feats,
    image_gain,
    image_bias,
    text_gain,
    text_bias,
    image_head,
    text_head,
    running_cov,
    pair_index,
):
    is_image = lax.axis_index("tower") == 0
    mp_index = lax.axis_index("mp")
    rows, image_width = image_feats.shape
    text_width = text_feats.shape[1]
    half = image_head.shape[1]
    width = running_cov.shape[1]
    dp_count = lax.axis_size("dp")
    total_rows = rows * dp_count

    text_head_padded = pad_rows(text_head, image_width)
    head_far = jnp.where(is_image, text_head_padded, image_head)
    head_own = jnp.where(is_image, image_head, text_head_padded)
    near, far = swap_halves(head_far)
    cov_old = flip(running_cov[0], "tower")

    def image_rows():
        return normalize(image_feats, image_gain, image_bias)

    def text_rows():
        standard, normed = normalize(text_feats, text_gain, text_bias)
        return pad_cols(standard, image_width), pad_cols(normed, image_width)

    standard, normed, normed_far = lax.cond(
        is_image,
        lambda: (*image_rows(), text_rows()[1]),
        lambda: (*text_rows(), image_rows()[1]),
    )
    projected = jnp.dot(normed, head_own, preferred_element_type=F32)
    head_other = jnp.concatenate([near, far], axis=0)
    head_full = jnp.where(
        mp_index == 0,
        jnp.concatenate([head_far, head_other], axis=1),
        jnp.concatenate([head_other, head_far], axis=1),
    )
    low_far = jnp.dot(normed_far, head_full, preferred_element_type=F32).astype(BF16)

    def panels_of(index):
        parts = []
        for col, row, count in PANELS[index]:
            parts.append(
                contract_rows(
                    low_far[:, row * BLOCK : (row + count) * BLOCK],
                    low_far[:, col * BLOCK : (col + 1) * BLOCK],
                )
            )
        return jnp.concatenate(parts, axis=0)

    cov_part = lax.cond(mp_index == 1, lambda: panels_of(1), lambda: panels_of(0))
    share = PANEL_ROWS // dp_count
    received = lax.all_to_all(
        cov_part.reshape(dp_count, share, BLOCK), "dp", 0, 0, tiled=True
    )
    cov_shard = jnp.sum(received, axis=0)
    gathered = lax.all_to_all(
        jnp.broadcast_to(cov_shard[None], (dp_count, share, BLOCK)), "dp", 0, 0, tiled=True
    ).reshape(PANEL_ROWS, BLOCK)
    other = jnp.concatenate(swap_halves(gathered), axis=0)
    lo = jnp.where(mp_index == 1, gathered, other)
    hi = jnp.where(mp_index == 1, other, gathered)
    inverse, cov_cols = inverse_factor(mp_index[None], lo, hi, cov_old, total_rows)
    new_cov = flip(cov_cols, "tower")
    inverse_rows = lax.dynamic_slice_in_dim(inverse, mp_index * half, half, 0)
    whitened = precise_dot(low_far.astype(F32), inverse_rows, ((1,), (1,))).astype(BF16)

    local_pairs = pair_index % rows
    places = jnp.arange(rows, dtype=jnp.int32)
    chosen = jnp.where(
        is_image, local_pairs[:, None] == places[None, :], places[:, None] == local_pairs[None, :]
    ).astype(BF16)
    targets = jnp.dot(chosen, whitened, preferred_element_type=F32)
    residual = projected - targets
    loss = jnp.sum(residual * residual) / (2.0 * total_rows * width)
    grad_low = (residual / width).astype(BF16)
    weight_grad = contract_rows(normed, grad_low)
    dnormed = lax.dot_general(
        grad_low, head_own, (((1,), (1,)), ((), ())), preferred_element_type=F32
    )
    norm_terms = jnp.stack([jnp.sum(standard * dnormed, axis=0), jnp.sum(dnormed, axis=0)])

    per_tower = (image_width + text_width) // 2
    chunk = per_tower // dp_count
    spill = flip(weight_grad[per_tower:], "tower")
    weight_part = jnp.where(
        is_image,
        weight_grad[:per_tower],
        jnp.concatenate([spill, weight_grad[:text_width]], axis=0),
    ).reshape(dp_count, chunk, half)
    weight_codes, weight_exps = to_fixed(weight_part, 1)
    norm_rows = norm_terms.reshape(-1, half)
    norm_codes, norm_exps = to_fixed(norm_rows, 0)
    loss_codes, loss_exps = to_fixed(jnp.broadcast_to(loss, (1, half)), 0)
    common = jnp.concatenate([norm_codes, norm_exps, loss_codes, loss_exps], axis=0)
    used = chunk + 1 + common.shape[0]
    payload = jnp.concatenate(
        [
            weight_codes,
            weight_exps,
            jnp.broadcast_to(common[None], (dp_count, *common.shape)),
            jnp.zeros((dp_count, -used % 8, half), jnp.int16),
        ],
        axis=1,
    )
    got = lax.all_to_all(payload, "dp", 0, 0, tiled=True)
    head_grads = jnp.sum(from_fixed(got[:, :chunk], got[:, chunk : chunk + 1]), axis=0)
    at = chunk + 1
    count = norm_rows.shape[0]
    norm_sum = jnp.sum(from_fixed(got[:, at : at + count], got[:, at + count : at + count + 1]), axis=0)
    at += count + 1
    loss_sum = jnp.sum(from_fixed(got[:, at : at + 1], got[:, at + 1 : at + 2]), axis=0)
    sums = jnp.concatenate([norm_sum, loss_sum], axis=0)
    mine = sums + flip(sums, "mp")
    theirs = flip(mine, "tower")
    image_sums = jnp.where(is_image, mine, theirs)
    text_sums = jnp.where(is_image, theirs, mine)
    image_norm = image_sums[:count].reshape(2, image_width)
    text_norm = text_sums[:count].reshape(2, image_width)[:, :text_width]
    norm_grads = jnp.concatenate([image_norm, text_norm], axis=1)
    losses = jnp.stack([image_sums[count, 0], text_sums[count, 0]])
    return new_cov[None], head_grads, norm_grads, losses


def solution(mesh):
    return jax.shard_map(
        body,
        mesh=mesh,
        in_specs=(
            P("dp", None),
            P("dp", None),
            P(),
            P(),
            P(),
            P(),
            P(None, "mp"),
            P(None, "mp"),
            P("tower", None, None),
            P("dp"),
        ),
        out_specs=(P("tower", None, "mp"), P(("tower", "dp"), "mp"), P(), P()),
        check_vma=False,
    )
```

```python
import jax
import jax.numpy as jnp
from jax import lax
from jax.experimental import pallas as pl
from jax.experimental.pallas import tpu as pltpu
from jax.sharding import PartitionSpec as P

EPSILON = 1e-05
F32 = jnp.float32
BF16 = jnp.bfloat16
BLOCK = 128
GROUP = 8
PANELS = {
    1: ((0, 0, 8), (1, 1, 7), (2, 2, 3)),
    0: ((2, 5, 3), (3, 3, 5), (4, 4, 4), (5, 5, 3), (6, 6, 2), (7, 7, 1)),
}
PRODUCTS = {
    1: (((0, 2), 0, (0, 1)), ((2, 3), 2, (2,))),
    0: (((2, 4), 3, (0, 1)), ((4, 6), 4, (2, 3)), ((6, 8), 6, (4, 5))),
}
PANEL_ROWS = 18 * BLOCK
WIDE = 2 * BLOCK
VMEM_LIMIT = 56 * 1024 * 1024


def flip(value, axis):
    return lax.ppermute(value, axis, [(0, 1), (1, 0)])


def swap_halves(value):
    dp_count = lax.axis_size("dp")
    x_hi_bit = 8 if dp_count == 64 else 1
    pairs = []
    for dp in range(dp_count):
        for mp in range(2):
            x_hi = (dp // x_hi_bit) % 2
            x = (x_hi * 2 + mp + (-1 if mp == 0 else 1)) % 4
            other = dp - x_hi * x_hi_bit + (x // 2) * x_hi_bit
            pairs.append((dp * 2 + mp, other * 2 + x % 2))
    half = value.shape[0] // 2
    near = flip(value[:half], "mp")
    far = lax.ppermute(value[half:], ("dp", "mp"), pairs)
    return near, far


def normalize(features, gain, bias):
    values = features.astype(F32)
    mean = jnp.mean(values, axis=1, keepdims=True)
    centered = values - mean
    var = jnp.mean(centered * centered, axis=1, keepdims=True)
    standard = centered * lax.rsqrt(var + EPSILON)
    return standard, (standard * gain[None, :] + bias[None, :]).astype(BF16)


def pad_cols(value, width):
    return jnp.pad(value, ((0, 0), (0, width - value.shape[1])))


def pad_rows(value, height):
    return jnp.pad(value, ((0, height - value.shape[0]), (0, 0)))


def contract_rows(a, b):
    return lax.dot_general(a, b, (((0,), (0,)), ((), ())), preferred_element_type=F32)


def precise_dot(a, b, dims):
    return lax.dot_general(
        a, b, (dims, ((), ())), precision=lax.Precision.HIGHEST, preferred_element_type=F32
    )


def factor_block(w_ref, t_ref):
    n = w_ref.shape[0]
    sub = lax.broadcasted_iota(jnp.int32, (GROUP, n), 0)
    lane = lax.broadcasted_iota(jnp.int32, (GROUP, n), 1)
    rows = [w_ref[GROUP * i : GROUP * (i + 1), :] for i in range(n // GROUP)]

    def spread(value):
        return jnp.broadcast_to(value, (GROUP, n))

    for g in range(n // GROUP):
        first = GROUP * g
        current = rows[g]
        inside = (lane >= first) & (lane < first + GROUP)
        cols = [spread(current[:, first + j : first + j + 1]) for j in range(GROUP)]
        full = jnp.where(inside, jnp.where(lane - first == sub, 1.0, 0.0), current)
        result = jnp.zeros((GROUP, n), F32)
        for j in range(GROUP):
            root = lax.rsqrt(spread(cols[j][j : j + 1, :]))
            recip = root * root
            here = sub == j
            row = spread(full[j : j + 1, :])
            result = jnp.where(here, row * root, result)
            scaled = row * recip
            full = jnp.where(here, scaled, full - cols[j] * scaled)
            for k in range(j + 1, GROUP):
                factor = spread(cols[k][j : j + 1, :]) * recip
                cols[k] = jnp.where(here, factor, cols[k] - cols[j] * factor)
        t_ref[first : first + GROUP, :] = jnp.where(lane < first + GROUP, result, 0.0)
        spreads = [spread(full[k : k + 1, :]) for k in range(GROUP)]
        for i in range(g + 1, n // GROUP):
            value = rows[i]
            terms = [
                spread(value[:, first + k : first + k + 1]) * spreads[k] for k in range(GROUP)
            ]
            while len(terms) > 1:
                terms = [terms[a] + terms[a + 1] for a in range(0, len(terms), 2)]
            rows[i] = jnp.where(inside, 0.0, value) - terms[0]


def covariance_kernel(mp_ref, normed_ref, own_ref, near_ref, far_ref, scale_ref, low_ref, out_ref, panel):
    depth, half = near_ref.shape
    other = jnp.dot(normed_ref[:, :depth], near_ref[...], preferred_element_type=F32)
    other += jnp.dot(normed_ref[:, depth:], far_ref[...], preferred_element_type=F32)
    other = (other.astype(BF16).astype(F32) * scale_ref[...]).astype(BF16)

    def products(index):
        low_ref[:, index * half : (index + 1) * half] = own_ref[...]
        low_ref[:, (1 - index) * half : (2 - index) * half] = other
        offsets = [0]
        for _, _, count in PANELS[index]:
            offsets.append(offsets[-1] + count * BLOCK)
        for (first, last), top, members in PRODUCTS[index]:
            bottom = max(PANELS[index][p][1] + PANELS[index][p][2] for p in members)
            product = contract_rows(
                low_ref[:, top * BLOCK : bottom * BLOCK], low_ref[:, first * BLOCK : last * BLOCK]
            )
            for p in members:
                col, row, count = PANELS[index][p]
                panel[offsets[p] : offsets[p + 1], :] = product[
                    (row - top) * BLOCK : (row - top + count) * BLOCK,
                    (col - first) * BLOCK : (col - first + 1) * BLOCK,
                ]

    for index in range(2):
        pl.when(mp_ref[0] == index)(lambda index=index: products(index))
    chunks, height, _ = out_ref.shape
    share = PANEL_ROWS // chunks
    panel[PANEL_ROWS:, :] = jnp.zeros((panel.shape[0] - PANEL_ROWS, BLOCK), F32)
    sub = lax.broadcasted_iota(jnp.int32, (height, BLOCK), 0)
    for c in range(chunks):
        value = panel[c * share : c * share + height, :]
        top = jnp.max(jnp.where(sub < share, jnp.abs(value), 0.0), axis=0, keepdims=True)
        exponent = jnp.ceil(jnp.log2(jnp.maximum(top, 1e-30)))
        codes = jnp.clip(jnp.round(value * jnp.exp2(15.0 - exponent)), -32767.0, 32767.0)
        codes = jnp.where(sub < share, codes, jnp.where(sub == share, exponent, 0.0))
        out_ref[c] = codes.astype(jnp.int32).astype(jnp.int16)


def covariance_part(mp_index, normed, own, near, far, scale, chunks):
    rows, half = own.shape
    share = PANEL_ROWS // chunks
    height = share + 8 - share % 8
    vmem = pl.BlockSpec(memory_space=pltpu.VMEM)
    return pl.pallas_call(
        covariance_kernel,
        out_shape=(
            jax.ShapeDtypeStruct((rows, 2 * half), BF16),
            jax.ShapeDtypeStruct((chunks, height, BLOCK), jnp.int16),
        ),
        in_specs=[pl.BlockSpec(memory_space=pltpu.SMEM)] + [vmem] * 5,
        out_specs=(vmem, vmem),
        scratch_shapes=[pltpu.VMEM((PANEL_ROWS + 8, BLOCK), F32)],
        compiler_params=pltpu.CompilerParams(vmem_limit_bytes=VMEM_LIMIT),
        cost_estimate=pl.CostEstimate(flops=3 * 10**9, bytes_accessed=10**7, transcendentals=0),
        name="covariance_part",
    )(mp_index, normed, own, near, far, scale)


def wide_factor(w_ref, k, blk, t, wide):
    a = pl.ds(pl.multiple_of(k * WIDE, WIDE), BLOCK)
    b = pl.ds(pl.multiple_of(k * WIDE + BLOCK, BLOCK), BLOCK)
    corner = w_ref[b, a]

    def half_step(h, carry):
        @pl.when(h == 0)
        def _():
            blk[...] = w_ref[a, a]

        @pl.when(h == 1)
        def _():
            first = t[...]
            wide[:BLOCK, :BLOCK] = first
            wide[:BLOCK, BLOCK:] = jnp.zeros((BLOCK, BLOCK), F32)
            left = precise_dot(corner, first, ((1,), (1,)))
            wide[BLOCK:, :BLOCK] = precise_dot(left, first, ((1,), (0,)))
            blk[...] = w_ref[b, b] - precise_dot(left, left, ((1,), (1,)))

        factor_block(blk, t)
        return carry

    lax.fori_loop(0, 2, half_step, 0)
    second = t[...]
    wide[BLOCK:, BLOCK:] = second
    wide[BLOCK:, :BLOCK] = -precise_dot(second, wide[BLOCK:, :BLOCK], ((1,), (0,)))


def load_panels(w, cov_row, old_ref, source, panels, scales, total_rows, pick=None):
    row_scale, col_scale = scales
    offset = 0
    for col, row, count in panels:
        there = slice(col * BLOCK, (col + 1) * BLOCK)
        for i in range(row, row + count):
            here = slice(i * BLOCK, (i + 1) * BLOCK)
            if pick is None or pick(i, col):
                both = row_scale[here, :] * col_scale[:, there]
                value = 0.5 * old_ref[here, there] * both
                value += (0.5 / total_rows) * source[offset : offset + BLOCK, :]
                w[here, there] = value
                if i > col:
                    w[there, here] = value.T
            offset += BLOCK


def first_kernel(total_rows, mp_ref, own_ref, old_ref, rs_ref, cs_ref, wide_ref, y_ref, w, blk, t):
    @pl.when(mp_ref[0] == 1)
    def _():
        load_panels(
            w, None, old_ref, own_ref, PANELS[1][:2], (rs_ref, cs_ref), total_rows
        )
        wide_factor(w, 0, blk, t, wide_ref)
        small = wide_ref[...]
        y_ref[:, WIDE:] = precise_dot(
            precise_dot(small, small, ((0,), (0,))), w[:WIDE, WIDE:], ((1,), (0,))
        )

    @pl.when(mp_ref[0] == 0)
    def _():
        wide_ref[...] = jnp.zeros(wide_ref.shape, F32)
        y_ref[...] = jnp.zeros(y_ref.shape, F32)


def second_kernel(
    total_rows, mp_ref, lo_ref, hi_ref, old_ref, rs_ref, cs_ref, wide_ref, y_ref,
    inv_ref, cov_ref, w, blk, t, wide, y,
):
    n = old_ref.shape[0]
    steps = n // WIDE
    scales = (rs_ref, cs_ref)
    load_panels(w, None, old_ref, lo_ref, PANELS[1], scales, total_rows)
    load_panels(w, None, old_ref, hi_ref, PANELS[0], scales, total_rows)
    half = cov_ref.shape[1]
    for index in range(2):
        @pl.when(mp_ref[0] == index)
        def _():
            cols = slice(index * half, (index + 1) * half)
            cov_ref[...] = w[:, cols] / rs_ref[...] / cs_ref[:, cols]

    mp = mp_ref[0]
    wide[...] = wide_ref[...]
    inv_ref[...] = jnp.zeros(inv_ref.shape, F32)

    def eliminate(k):
        first, last = k * WIDE, (k + 1) * WIDE
        small = wide[...]
        inv_ref[first:last, first:last] = small
        gram = precise_dot(small, small, ((0,), (0,)))
        if k > 0:
            left = w[first:last, :first]
            inv_ref[first:last, :first] = precise_dot(small, left, ((1,), (0,)))
            y[:, :first] = precise_dot(gram, left, ((1,), (0,)))
        y[:, first:last] = gram
        if last < n:
            right = w[first:last, last:]
            if k > 0:
                y[:, last:] = precise_dot(gram, right, ((1,), (0,)))
            else:
                @pl.when(mp == 0)
                def _():
                    y[:, last:] = precise_dot(gram, right, ((1,), (0,)))

                @pl.when(mp == 1)
                def _():
                    y[:, last:] = y_ref[:, last:]
            below = w[last:, first:last]
            if k > 0:
                w[last:, :first] -= precise_dot(below, y[:, :first], ((1,), (0,)))
            w[last:, last:] -= precise_dot(below, y[:, last:], ((1,), (0,)))
            w[last:, first:last] = -precise_dot(below, y[:, first:last], ((1,), (0,)))

    def step(k, carry):
        @pl.when((k > 0) | (mp == 0))
        def _():
            wide_factor(w, k, blk, t, wide)

        for index in range(steps):
            pl.when(k == index)(lambda index=index: eliminate(index))
        return carry

    lax.fori_loop(0, jnp.where(mp == 0, steps // 2, steps), step, 0)


def first_factor(mp_index, own, cov_old, row_scale, col_scale, total_rows):
    n = cov_old.shape[0]
    vmem = pl.BlockSpec(memory_space=pltpu.VMEM)

    def kernel(*refs):
        first_kernel(total_rows, *refs)

    return pl.pallas_call(
        kernel,
        out_shape=(
            jax.ShapeDtypeStruct((WIDE, WIDE), F32),
            jax.ShapeDtypeStruct((WIDE, n), F32),
        ),
        in_specs=[pl.BlockSpec(memory_space=pltpu.SMEM)] + [vmem] * 4,
        out_specs=(vmem, vmem),
        scratch_shapes=[
            pltpu.VMEM((n, n), F32),
            pltpu.VMEM((BLOCK, BLOCK), F32),
            pltpu.VMEM((BLOCK, BLOCK), F32),
        ],
        compiler_params=pltpu.CompilerParams(vmem_limit_bytes=VMEM_LIMIT),
        cost_estimate=pl.CostEstimate(flops=15 * 10**9, bytes_accessed=10**7, transcendentals=0),
        name="first_factor",
    )(mp_index, own, cov_old, row_scale, col_scale)


def second_factor(mp_index, lo, hi, cov_old, row_scale, col_scale, wide, y, total_rows):
    n = cov_old.shape[0]
    vmem = pl.BlockSpec(memory_space=pltpu.VMEM)

    def kernel(*refs):
        second_kernel(total_rows, *refs)

    return pl.pallas_call(
        kernel,
        out_shape=(
            jax.ShapeDtypeStruct((n, n), F32),
            jax.ShapeDtypeStruct((n, n // 2), F32),
        ),
        in_specs=[pl.BlockSpec(memory_space=pltpu.SMEM)] + [vmem] * 7,
        out_specs=(vmem, vmem),
        scratch_shapes=[
            pltpu.VMEM((n, n), F32),
            pltpu.VMEM((BLOCK, BLOCK), F32),
            pltpu.VMEM((BLOCK, BLOCK), F32),
            pltpu.VMEM((WIDE, WIDE), F32),
            pltpu.VMEM((WIDE, n), F32),
        ],
        compiler_params=pltpu.CompilerParams(vmem_limit_bytes=VMEM_LIMIT),
        cost_estimate=pl.CostEstimate(flops=50 * 10**9, bytes_accessed=2 * 10**7, transcendentals=0),
        name="second_factor",
    )(mp_index, lo, hi, cov_old, row_scale, col_scale, wide, y)


def gather_dp(shard):
    dp_count = lax.axis_size("dp")
    along = min(8, dp_count)
    across = dp_count // along
    rows = shard.shape[0]
    z_groups = [[a * along + z for z in range(along)] for a in range(across)]
    yx_groups = [[a * along + z for a in range(across)] for z in range(along)]
    padded = jnp.pad(shard, ((0, -rows % 8), (0, 0)))
    value = lax.all_to_all(
        jnp.broadcast_to(padded[None], (along, *padded.shape)),
        "dp", 0, 0, tiled=True, axis_index_groups=z_groups,
    )[:, :rows].reshape(along * rows, -1)
    if across > 1:
        value = lax.all_to_all(
            jnp.broadcast_to(value[None], (across, *value.shape)),
            "dp", 0, 0, tiled=True, axis_index_groups=yx_groups,
        ).reshape(dp_count * rows, -1)
    return value


def fixed_scale(exponent):
    return jnp.exp2(exponent - 15.0)


def to_fixed(value, axis):
    top = jnp.maximum(jnp.max(jnp.abs(value), axis=axis, keepdims=True), 1e-30)
    exponent = jnp.ceil(jnp.log2(top))
    codes = jnp.clip(jnp.round(value / fixed_scale(exponent)), -32767.0, 32767.0)
    return codes.astype(jnp.int16), exponent.astype(jnp.int16)


def from_fixed(codes, exponent):
    return codes.astype(F32) * fixed_scale(exponent.astype(F32))


def body(
    image_feats,
    text_feats,
    image_gain,
    image_bias,
    text_gain,
    text_bias,
    image_head,
    text_head,
    running_cov,
    pair_index,
):
    is_image = lax.axis_index("tower") == 0
    mp_index = lax.axis_index("mp")
    rows, image_width = image_feats.shape
    text_width = text_feats.shape[1]
    half = image_head.shape[1]
    width = running_cov.shape[1]
    dp_count = lax.axis_size("dp")
    total_rows = rows * dp_count

    text_head_padded = pad_rows(text_head, image_width)
    head_far = jnp.where(is_image, text_head_padded, image_head)
    head_own = jnp.where(is_image, image_head, text_head_padded)
    near, far = swap_halves(head_far)
    cov_old = flip(running_cov[0], "tower")

    def image_rows():
        return normalize(image_feats, image_gain, image_bias)

    def text_rows():
        standard, normed = normalize(text_feats, text_gain, text_bias)
        return pad_cols(standard, image_width), pad_cols(normed, image_width)

    standard, normed, normed_far = lax.cond(
        is_image,
        lambda: (*image_rows(), text_rows()[1]),
        lambda: (*text_rows(), image_rows()[1]),
    )
    projected = jnp.dot(normed, head_own, preferred_element_type=F32)

    gain_far = jnp.where(is_image, jnp.pad(text_gain, (0, image_width - text_width)), image_gain)
    bias_far = jnp.where(is_image, jnp.pad(text_bias, (0, image_width - text_width)), image_bias)
    head_wide = head_far.astype(F32)
    spread = jnp.sum((gain_far[:, None] * head_wide) ** 2, axis=0)
    middle = jnp.sum(bias_far[:, None] * head_wide, axis=0)
    size = jnp.maximum(spread + middle * middle, 1e-30)
    scale_own = jnp.exp2(-jnp.round(0.5 * jnp.log2(size)))
    scale_other = flip(scale_own, "mp")
    scales = jnp.where(
        mp_index == 0,
        jnp.concatenate([scale_own, scale_other]),
        jnp.concatenate([scale_other, scale_own]),
    )
    own_low = jnp.dot(normed_far, head_far, preferred_element_type=F32).astype(BF16)
    own_low = (own_low.astype(F32) * scale_own[None, :]).astype(BF16)
    mp_scalar = mp_index[None].astype(jnp.int32)
    low_far, cov_codes = covariance_part(
        mp_scalar, normed_far, own_low, near, far, scale_other[None, :], dp_count
    )
    share = PANEL_ROWS // dp_count
    received = lax.all_to_all(cov_codes, "dp", 0, 0, tiled=True)
    cov_shard = jnp.sum(
        from_fixed(received[:, :share], received[:, share : share + 1]), axis=0
    )
    gathered = gather_dp(cov_shard)
    near_panels, far_panels = swap_halves(gathered)
    row_scale, col_scale = scales[:, None], scales[None, :]
    wide, y = first_factor(mp_scalar, gathered, cov_old, row_scale, col_scale, total_rows)
    other = jnp.concatenate([near_panels, far_panels], axis=0)
    lo = jnp.where(mp_index == 1, gathered, other)
    hi = jnp.where(mp_index == 1, other, gathered)
    inverse, cov_cols = second_factor(
        mp_scalar, lo, hi, cov_old, row_scale, col_scale, wide, y, total_rows
    )
    new_cov = flip(cov_cols, "tower")
    inverse_rows = lax.dynamic_slice_in_dim(inverse, mp_index * half, half, 0)
    whitened = precise_dot(low_far.astype(F32), inverse_rows, ((1,), (1,))).astype(BF16)

    local_pairs = pair_index % rows
    places = jnp.arange(rows, dtype=jnp.int32)
    chosen = jnp.where(
        is_image, local_pairs[:, None] == places[None, :], places[:, None] == local_pairs[None, :]
    ).astype(BF16)
    targets = jnp.dot(chosen, whitened, preferred_element_type=F32)
    residual = projected - targets
    loss = jnp.sum(residual * residual) / (2.0 * total_rows * width)
    grad_low = (residual / width).astype(BF16)
    weight_grad = contract_rows(normed, grad_low)
    dnormed = lax.dot_general(
        grad_low, head_own, (((1,), (1,)), ((), ())), preferred_element_type=F32
    )
    norm_terms = jnp.stack([jnp.sum(standard * dnormed, axis=0), jnp.sum(dnormed, axis=0)])

    per_tower = (image_width + text_width) // 2
    chunk = per_tower // dp_count
    spill = flip(weight_grad[per_tower:], "tower")
    weight_part = jnp.where(
        is_image,
        weight_grad[:per_tower],
        jnp.concatenate([spill, weight_grad[:text_width]], axis=0),
    ).reshape(dp_count, chunk, half)
    weight_codes, weight_exps = to_fixed(weight_part, 1)
    norm_rows = norm_terms.reshape(-1, half)
    norm_codes, norm_exps = to_fixed(norm_rows, 0)
    loss_codes, loss_exps = to_fixed(jnp.broadcast_to(loss, (1, half)), 0)
    common = jnp.concatenate([norm_codes, norm_exps, loss_codes, loss_exps], axis=0)
    used = chunk + 1 + common.shape[0]
    payload = jnp.concatenate(
        [
            weight_codes,
            weight_exps,
            jnp.broadcast_to(common[None], (dp_count, *common.shape)),
            jnp.zeros((dp_count, -used % 8, half), jnp.int16),
        ],
        axis=1,
    )
    got = lax.all_to_all(payload, "dp", 0, 0, tiled=True)
    head_grads = jnp.sum(from_fixed(got[:, :chunk], got[:, chunk : chunk + 1]), axis=0)
    at = chunk + 1
    count = norm_rows.shape[0]
    norm_sum = jnp.sum(from_fixed(got[:, at : at + count], got[:, at + count : at + count + 1]), axis=0)
    at += count + 1
    loss_sum = jnp.sum(from_fixed(got[:, at : at + 1], got[:, at + 1 : at + 2]), axis=0)
    sums = jnp.concatenate([norm_sum, loss_sum], axis=0)
    mine = sums + flip(sums, "mp")
    theirs = flip(mine, "tower")
    image_sums = jnp.where(is_image, mine, theirs)
    text_sums = jnp.where(is_image, theirs, mine)
    image_norm = image_sums[:count].reshape(2, image_width)
    text_norm = text_sums[:count].reshape(2, image_width)[:, :text_width]
    norm_grads = jnp.concatenate([image_norm, text_norm], axis=1)
    losses = jnp.stack([image_sums[count, 0], text_sums[count, 0]])
    return new_cov[None], head_grads, norm_grads, losses


def solution(mesh):
    return jax.shard_map(
        body,
        mesh=mesh,
        in_specs=(
            P("dp", None),
            P("dp", None),
            P(),
            P(),
            P(),
            P(),
            P(None, "mp"),
            P(None, "mp"),
            P("tower", None, None),
            P("dp"),
        ),
        out_specs=(P("tower", None, "mp"), P(("tower", "dp"), "mp"), P(), P()),
        check_vma=False,
    )
```

```python
import jax
import jax.numpy as jnp
from jax import lax
from jax.experimental import pallas as pl
from jax.experimental.pallas import tpu as pltpu
from jax.sharding import PartitionSpec as P

EPSILON = 1e-05
F32 = jnp.float32
BF16 = jnp.bfloat16
BLOCK = 128
GROUP = 8
PANELS = {
    1: ((0, 0, 8), (1, 1, 7), (2, 2, 3)),
    0: ((2, 5, 3), (3, 3, 5), (4, 4, 4), (5, 5, 3), (6, 6, 2), (7, 7, 1)),
}
PRODUCTS = {
    1: (((0, 2), 0, (0, 1)), ((2, 3), 2, (2,))),
    0: (((2, 4), 3, (0, 1)), ((4, 6), 4, (2, 3)), ((6, 8), 6, (4, 5))),
}
PANEL_ROWS = 18 * BLOCK
WIDE = 2 * BLOCK
VMEM_LIMIT = 56 * 1024 * 1024


def flip(value, axis):
    return lax.ppermute(value, axis, [(0, 1), (1, 0)])


def swap_halves(value):
    dp_count = lax.axis_size("dp")
    x_hi_bit = 8 if dp_count == 64 else 1
    pairs = []
    for dp in range(dp_count):
        for mp in range(2):
            x_hi = (dp // x_hi_bit) % 2
            x = (x_hi * 2 + mp + (-1 if mp == 0 else 1)) % 4
            other = dp - x_hi * x_hi_bit + (x // 2) * x_hi_bit
            pairs.append((dp * 2 + mp, other * 2 + x % 2))
    half = value.shape[0] // 2
    near = flip(value[:half], "mp")
    far = lax.ppermute(value[half:], ("dp", "mp"), pairs)
    return near, far


def normalize(features, gain, bias):
    values = features.astype(F32)
    mean = jnp.mean(values, axis=1, keepdims=True)
    centered = values - mean
    var = jnp.mean(centered * centered, axis=1, keepdims=True)
    standard = centered * lax.rsqrt(var + EPSILON)
    return standard, (standard * gain[None, :] + bias[None, :]).astype(BF16)


def pad_cols(value, width):
    return jnp.pad(value, ((0, 0), (0, width - value.shape[1])))


def pad_rows(value, height):
    return jnp.pad(value, ((0, height - value.shape[0]), (0, 0)))


def contract_rows(a, b):
    return lax.dot_general(a, b, (((0,), (0,)), ((), ())), preferred_element_type=F32)


def precise_dot(a, b, dims):
    return lax.dot_general(
        a, b, (dims, ((), ())), precision=lax.Precision.HIGHEST, preferred_element_type=F32
    )


def tree_sum(terms):
    terms = list(terms)
    while len(terms) > 1:
        terms = [
            terms[a] + terms[a + 1] if a + 1 < len(terms) else terms[a]
            for a in range(0, len(terms), 2)
        ]
    return terms[0]


def factor_block(w_ref, t_ref):
    n = w_ref.shape[0]
    sub = lax.broadcasted_iota(jnp.int32, (GROUP, n), 0)
    lane = lax.broadcasted_iota(jnp.int32, (GROUP, n), 1)
    rows = [w_ref[GROUP * i : GROUP * (i + 1), :] for i in range(n // GROUP)]

    def spread(value):
        return jnp.broadcast_to(value, (GROUP, n))

    for g in range(n // GROUP):
        first = GROUP * g
        inside = (lane >= first) & (lane < first + GROUP)
        cols = [spread(rows[g][:, first + j : first + j + 1]) for j in range(GROUP)]
        e = [[spread(cols[j][i : i + 1, :]) for j in range(i + 1)] for i in range(GROUP)]
        full = jnp.where(inside, jnp.where(lane - first == sub, 1.0, 0.0), rows[g])
        right = [spread(full[k : k + 1, :]) for k in range(GROUP)]
        low = [[None] * GROUP for _ in range(GROUP)]
        roots, upper = [], []
        for j in range(GROUP):
            root = lax.rsqrt(e[j][j])
            roots.append(root)
            upper.append(right[j] * root)
            for i in range(j + 1, GROUP):
                low[i][j] = e[i][j] * root
            for k in range(j + 1, GROUP):
                right[k] = right[k] - low[k][j] * upper[j]
                for i in range(k, GROUP):
                    e[i][k] = e[i][k] - low[i][j] * low[k][j]
        result = upper[-1]
        for j in range(GROUP - 1):
            result = jnp.where(sub == j, upper[j], result)
        t_ref[first : first + GROUP, :] = jnp.where(lane < first + GROUP, result, 0.0)
        for i in range(g + 1, n // GROUP):
            left = []
            for j in range(GROUP):
                entry = spread(rows[i][:, first + j : first + j + 1])
                for k in range(j):
                    entry = entry - left[k] * low[j][k]
                left.append(entry * roots[j])
            rows[i] = jnp.where(inside, 0.0, rows[i]) - tree_sum(
                left[k] * upper[k] for k in range(GROUP)
            )


def covariance_kernel(mp_ref, normed_ref, own_ref, near_ref, far_ref, scale_ref, low_ref, out_ref, panel):
    depth, half = near_ref.shape
    other = jnp.dot(normed_ref[:, :depth], near_ref[...], preferred_element_type=F32)
    other += jnp.dot(normed_ref[:, depth:], far_ref[...], preferred_element_type=F32)
    other = (other.astype(BF16).astype(F32) * scale_ref[...]).astype(BF16)

    def products(index):
        low_ref[:, index * half : (index + 1) * half] = own_ref[...]
        low_ref[:, (1 - index) * half : (2 - index) * half] = other
        offsets = [0]
        for _, _, count in PANELS[index]:
            offsets.append(offsets[-1] + count * BLOCK)
        for (first, last), top, members in PRODUCTS[index]:
            bottom = max(PANELS[index][p][1] + PANELS[index][p][2] for p in members)
            product = contract_rows(
                low_ref[:, top * BLOCK : bottom * BLOCK], low_ref[:, first * BLOCK : last * BLOCK]
            )
            for p in members:
                col, row, count = PANELS[index][p]
                panel[offsets[p] : offsets[p + 1], :] = product[
                    (row - top) * BLOCK : (row - top + count) * BLOCK,
                    (col - first) * BLOCK : (col - first + 1) * BLOCK,
                ]

    for index in range(2):
        pl.when(mp_ref[0] == index)(lambda index=index: products(index))
    chunks, height, _ = out_ref.shape
    share = PANEL_ROWS // chunks
    panel[PANEL_ROWS:, :] = jnp.zeros((panel.shape[0] - PANEL_ROWS, BLOCK), F32)
    sub = lax.broadcasted_iota(jnp.int32, (height, BLOCK), 0)
    for c in range(chunks):
        value = panel[c * share : c * share + height, :]
        top = jnp.max(jnp.where(sub < share, jnp.abs(value), 0.0), axis=0, keepdims=True)
        exponent = jnp.ceil(jnp.log2(jnp.maximum(top, 1e-30)))
        codes = jnp.clip(jnp.round(value * jnp.exp2(15.0 - exponent)), -32767.0, 32767.0)
        codes = jnp.where(sub < share, codes, jnp.where(sub == share, exponent, 0.0))
        out_ref[c] = codes.astype(jnp.int32).astype(jnp.int16)


def covariance_part(mp_index, normed, own, near, far, scale, chunks):
    rows, half = own.shape
    share = PANEL_ROWS // chunks
    height = share + 8 - share % 8
    vmem = pl.BlockSpec(memory_space=pltpu.VMEM)
    return pl.pallas_call(
        covariance_kernel,
        out_shape=(
            jax.ShapeDtypeStruct((rows, 2 * half), BF16),
            jax.ShapeDtypeStruct((chunks, height, BLOCK), jnp.int16),
        ),
        in_specs=[pl.BlockSpec(memory_space=pltpu.SMEM)] + [vmem] * 5,
        out_specs=(vmem, vmem),
        scratch_shapes=[pltpu.VMEM((PANEL_ROWS + 8, BLOCK), F32)],
        compiler_params=pltpu.CompilerParams(vmem_limit_bytes=VMEM_LIMIT),
        cost_estimate=pl.CostEstimate(flops=3 * 10**9, bytes_accessed=10**7, transcendentals=0),
        name="covariance_part",
    )(mp_index, normed, own, near, far, scale)


def wide_factor(w_ref, k, blk, t, wide):
    a = pl.ds(pl.multiple_of(k * WIDE, WIDE), BLOCK)
    b = pl.ds(pl.multiple_of(k * WIDE + BLOCK, BLOCK), BLOCK)
    corner = w_ref[b, a]

    def half_step(h, carry):
        @pl.when(h == 0)
        def _():
            blk[...] = w_ref[a, a]

        @pl.when(h == 1)
        def _():
            first = t[...]
            wide[:BLOCK, :BLOCK] = first
            wide[:BLOCK, BLOCK:] = jnp.zeros((BLOCK, BLOCK), F32)
            left = precise_dot(corner, first, ((1,), (1,)))
            wide[BLOCK:, :BLOCK] = precise_dot(left, first, ((1,), (0,)))
            blk[...] = w_ref[b, b] - precise_dot(left, left, ((1,), (1,)))

        factor_block(blk, t)
        return carry

    lax.fori_loop(0, 2, half_step, 0)
    second = t[...]
    wide[BLOCK:, BLOCK:] = second
    wide[BLOCK:, :BLOCK] = -precise_dot(second, wide[BLOCK:, :BLOCK], ((1,), (0,)))


def load_panels(w, old_ref, source, panels, scales, total_rows):
    row_scale, col_scale = scales
    offset = 0
    for col, row, count in panels:
        there = slice(col * BLOCK, (col + 1) * BLOCK)
        for i in range(row, row + count):
            here = slice(i * BLOCK, (i + 1) * BLOCK)
            both = row_scale[here, :] * col_scale[:, there]
            value = 0.5 * old_ref[here, there] * both
            value += (0.5 / total_rows) * source(offset)
            w[here, there] = value
            if i > col:
                w[there, here] = value.T
            offset += BLOCK


def eliminate(k, w, u, small):
    first, last = k * WIDE, (k + 1) * WIDE
    n = w.shape[1]
    if first > 0:
        u[:, :first] = precise_dot(small, w[first:last, :first], ((1,), (0,)))
    u[:, first:last] = small
    if last < n:
        u[:, last:] = precise_dot(small, w[first:last, last:], ((1,), (0,)))


def update_below(k, w, u, small):
    first, last = k * WIDE, (k + 1) * WIDE
    left = precise_dot(w[last:, first:last], small, ((1,), (1,)))
    w[last:, first:last] = jnp.zeros((w.shape[0] - last, WIDE), F32)
    w[last:, :] -= precise_dot(left, u[...], ((1,), (0,)))


def first_kernel(total_rows, mp_ref, own_ref, old_ref, rs_ref, cs_ref, wide_ref, u_ref, w, blk, t):
    @pl.when(mp_ref[0] == 1)
    def _():
        def own(offset):
            return own_ref[offset : offset + BLOCK, :]

        load_panels(w, old_ref, own, PANELS[1][:2], (rs_ref, cs_ref), total_rows)
        wide_factor(w, 0, blk, t, wide_ref)
        eliminate(0, w, u_ref, wide_ref[...])

    @pl.when(mp_ref[0] == 0)
    def _():
        wide_ref[...] = jnp.zeros(wide_ref.shape, F32)
        u_ref[...] = jnp.zeros(u_ref.shape, F32)


def second_kernel(
    total_rows, mp_ref, own_ref, near_ref, far_ref, old_ref, rs_ref, cs_ref, wide_ref, u_ref,
    inv_ref, cov_ref, w, blk, t, wide, u,
):
    n = old_ref.shape[0]
    half = cov_ref.shape[1]
    steps = n // WIDE
    scales = (rs_ref, cs_ref)
    mp = mp_ref[0]
    split = near_ref.shape[0]

    def own(offset):
        return own_ref[offset : offset + BLOCK, :]

    def other(offset):
        if offset < split:
            return near_ref[offset : offset + BLOCK, :]
        return far_ref[offset - split : offset - split + BLOCK, :]

    def covariance_columns(index):
        for source, panels in ((own, PANELS[index]), (other, PANELS[1 - index])):
            offset = 0
            for col, row, count in panels:
                for i in range(row, row + count):
                    value = source(offset) * (0.5 / total_rows)
                    offset += BLOCK
                    for r, c in ((i, col),) if i == col else ((i, col), (col, i)):
                        if c * BLOCK // half != index:
                            continue
                        block = value if r == i else value.T
                        here = slice(r * BLOCK, (r + 1) * BLOCK)
                        there = slice(c * BLOCK, (c + 1) * BLOCK)
                        at = slice(c * BLOCK - index * half, (c + 1) * BLOCK - index * half)
                        cov_ref[here, at] = block / rs_ref[here, :] / cs_ref[:, there]

    for index in range(2):
        @pl.when(mp == index)
        def _():
            load_panels(w, old_ref, own, PANELS[index], scales, total_rows)
            load_panels(w, old_ref, other, PANELS[1 - index], scales, total_rows)
            covariance_columns(index)

    wide[...] = wide_ref[...]
    u[...] = u_ref[...]

    def step(k, carry):
        @pl.when((k > 0) | (mp == 0))
        def _():
            wide_factor(w, k, blk, t, wide)

        def whole_step(index):
            small = wide[...]
            if index > 0:
                eliminate(index, w, u, small)
            else:
                @pl.when(mp == 0)
                def _():
                    eliminate(index, w, u, small)

            @pl.when(mp == index * WIDE // half)
            def _():
                here = slice(index * WIDE % half, index * WIDE % half + WIDE)
                last = (index + 1) * WIDE
                inv_ref[here, :last] = u[:, :last]
                if last < n:
                    inv_ref[here, last:] = jnp.zeros((WIDE, n - last), F32)

            if index + 1 < steps:
                update_below(index, w, u, small)

        for index in range(steps):
            pl.when(k == index)(lambda index=index: whole_step(index))
        return carry

    lax.fori_loop(0, jnp.where(mp == 0, half // WIDE, steps), step, 0)


def first_factor(mp_index, own, cov_old, row_scale, col_scale, total_rows):
    n = cov_old.shape[0]
    vmem = pl.BlockSpec(memory_space=pltpu.VMEM)

    def kernel(*refs):
        first_kernel(total_rows, *refs)

    return pl.pallas_call(
        kernel,
        out_shape=(
            jax.ShapeDtypeStruct((WIDE, WIDE), F32),
            jax.ShapeDtypeStruct((WIDE, n), F32),
        ),
        in_specs=[pl.BlockSpec(memory_space=pltpu.SMEM)] + [vmem] * 4,
        out_specs=(vmem, vmem),
        scratch_shapes=[
            pltpu.VMEM((n, n), F32),
            pltpu.VMEM((BLOCK, BLOCK), F32),
            pltpu.VMEM((BLOCK, BLOCK), F32),
        ],
        compiler_params=pltpu.CompilerParams(vmem_limit_bytes=VMEM_LIMIT),
        cost_estimate=pl.CostEstimate(flops=15 * 10**9, bytes_accessed=10**7, transcendentals=0),
        name="first_factor",
    )(mp_index, own, cov_old, row_scale, col_scale)


def second_factor(mp_index, own, near, far, cov_old, row_scale, col_scale, wide, u, total_rows):
    n = cov_old.shape[0]
    vmem = pl.BlockSpec(memory_space=pltpu.VMEM)

    def kernel(*refs):
        second_kernel(total_rows, *refs)

    return pl.pallas_call(
        kernel,
        out_shape=(
            jax.ShapeDtypeStruct((n // 2, n), F32),
            jax.ShapeDtypeStruct((n, n // 2), F32),
        ),
        in_specs=[pl.BlockSpec(memory_space=pltpu.SMEM)] + [vmem] * 8,
        out_specs=(vmem, vmem),
        scratch_shapes=[
            pltpu.VMEM((n, n), F32),
            pltpu.VMEM((BLOCK, BLOCK), F32),
            pltpu.VMEM((BLOCK, BLOCK), F32),
            pltpu.VMEM((WIDE, WIDE), F32),
            pltpu.VMEM((WIDE, n), F32),
        ],
        compiler_params=pltpu.CompilerParams(vmem_limit_bytes=VMEM_LIMIT),
        cost_estimate=pl.CostEstimate(flops=50 * 10**9, bytes_accessed=2 * 10**7, transcendentals=0),
        name="second_factor",
    )(mp_index, own, near, far, cov_old, row_scale, col_scale, wide, u)


def residual_kernel(
    total_rows, image_ref, inv_ref, low_ref, proj_ref, row_ref, col_ref, head_ref, standard_ref,
    normed_ref, grad_ref, sums_ref, spill_ref, white,
):
    rows, half = proj_ref.shape
    width = low_ref.shape[1]
    left = inv_ref[...]
    high = left.astype(BF16)
    left = left - high.astype(F32)
    middle = left.astype(BF16)
    small = (left - middle.astype(F32)).astype(BF16)
    dims = (((1,), (1,)), ((), ()))
    tile = 256
    for r in range(0, rows, tile):
        low = low_ref[r : r + tile, :]
        value = lax.dot_general(low, small, dims, preferred_element_type=F32)
        value += lax.dot_general(low, middle, dims, preferred_element_type=F32)
        value += lax.dot_general(low, high, dims, preferred_element_type=F32)
        white[r : r + tile, :] = value.astype(BF16)
    is_image = image_ref[0] == 1
    lane = lax.broadcasted_iota(jnp.int32, (tile, rows), 1)
    sub = lax.broadcasted_iota(jnp.int32, (tile, rows), 0)
    wanted = jnp.where(is_image, 1, 0)
    gain = jnp.zeros((1, width), F32)
    shift = jnp.zeros((1, width), F32)
    total = jnp.zeros((1, half), F32)
    for r in range(0, rows, tile):
        from_image = jnp.where(col_ref[r : r + tile, :] == lane, wanted, 0)
        from_text = jnp.where(row_ref[...] == sub + r, 1 - wanted, 0)
        chosen = (from_image + from_text).astype(F32).astype(BF16)
        targets = jnp.dot(chosen, white[...], preferred_element_type=F32)
        residual = proj_ref[r : r + tile, :] - targets
        total += jnp.sum(residual * residual, axis=0, keepdims=True)
        grad = (residual * (1.0 / width)).astype(BF16)
        grad_ref[r : r + tile, :] = grad
        dnormed = lax.dot_general(grad, head_ref[...], dims, preferred_element_type=F32)
        gain += jnp.sum(standard_ref[r : r + tile, :] * dnormed, axis=0, keepdims=True)
        shift += jnp.sum(dnormed, axis=0, keepdims=True)
    sums_ref[0:1, :] = gain
    sums_ref[1:2, :] = shift
    loss_value = jnp.sum(total, axis=1, keepdims=True) / (2.0 * total_rows * width)
    sums_ref[2:8, :] = jnp.broadcast_to(loss_value, (6, width))
    kept = width - spill_ref.shape[0]
    spill_ref[...] = contract_rows(normed_ref[:, kept:], grad_ref[...])


def residual_part(is_image, inverse, low, projected, pairs, head, standard, normed, spilled, total_rows):
    rows, half = projected.shape
    width = low.shape[1]
    vmem = pl.BlockSpec(memory_space=pltpu.VMEM)

    def kernel(*refs):
        residual_kernel(total_rows, *refs)

    return pl.pallas_call(
        kernel,
        out_shape=(
            jax.ShapeDtypeStruct((rows, half), BF16),
            jax.ShapeDtypeStruct((8, width), F32),
            jax.ShapeDtypeStruct((spilled, half), F32),
        ),
        in_specs=[pl.BlockSpec(memory_space=pltpu.SMEM)] + [vmem] * 8,
        out_specs=(vmem, vmem, vmem),
        scratch_shapes=[pltpu.VMEM((rows, half), BF16)],
        compiler_params=pltpu.CompilerParams(vmem_limit_bytes=VMEM_LIMIT),
        cost_estimate=pl.CostEstimate(flops=6 * 10**9, bytes_accessed=2 * 10**7, transcendentals=0),
        name="residual_part",
    )(is_image, inverse, low, projected, pairs[None, :], pairs[:, None], head, standard, normed)


CHUNK_EXPONENT, NORM_EXPONENT, LOSS_EXPONENTS, LOSS_CODES = 384, 385, 386, 388


def exponent_of(value):
    return jnp.ceil(jnp.log2(jnp.maximum(jnp.abs(value), 1e-30)))


def codes_of(value, exponent):
    return jnp.clip(jnp.round(value * jnp.exp2(15.0 - exponent)), -32767.0, 32767.0)


def payload_kernel(
    text_width, place_ref, weight_ref, spill_ref, mine_ref, mp_ref, tower_ref, both_ref,
    out_ref, part, image, text, first, second,
):
    chunks, height, half = out_ref.shape
    spilled = spill_ref.shape[0]
    kept = weight_ref.shape[0] - spilled
    share = kept // chunks
    width = mine_ref.shape[1]
    place = place_ref[0]
    mine = mine_ref[...] + mp_ref[...]
    theirs = tower_ref[...] + both_ref[...]

    @pl.when(place < 2)
    def _():
        part[:kept, :] = weight_ref[:kept, :]
        image[...] = mine
        text[...] = theirs

    @pl.when(place >= 2)
    def _():
        part[:spilled, :] = spill_ref[...]
        part[spilled:kept, :] = weight_ref[: kept - spilled, :]
        image[...] = theirs
        text[...] = mine

    part[kept:, :] = jnp.zeros((part.shape[0] - kept, half), F32)
    second[...] = jnp.zeros(second.shape, F32)
    quarter = (width + text_width) // 2
    for index in range(4):
        @pl.when(place == index)
        def _():
            row = slice(index // 2, index // 2 + 1)
            pieces = [(image, c) for c in range(0, width, BLOCK)]
            pieces += [(text, c) for c in range(0, text_width, BLOCK)]
            start = (index % 2) * quarter // BLOCK
            for i, (ref, c) in enumerate(pieces[start : start + quarter // BLOCK]):
                if i * BLOCK < half:
                    first[:, i * BLOCK : (i + 1) * BLOCK] = ref[row, c : c + BLOCK]
                else:
                    at = i * BLOCK - half
                    second[:, at : at + BLOCK] = ref[row, c : c + BLOCK]

    lane = lax.broadcasted_iota(jnp.int32, (1, half), 1)
    top = jnp.maximum(
        jnp.max(jnp.abs(first[...]), axis=1, keepdims=True),
        jnp.max(jnp.abs(second[...]), axis=1, keepdims=True),
    )
    norm_exponent = exponent_of(top)
    loss = jnp.where(lane % 2 == 0, image[2:3, :half], text[2:3, :half])
    loss_exponent = exponent_of(loss)
    tail = jnp.where(lane < LOSS_CODES, loss_exponent, codes_of(loss, loss_exponent))
    tail = jnp.where(lane == NORM_EXPONENT, norm_exponent, tail)
    tail = jnp.where(lane < CHUNK_EXPONENT, codes_of(second[...], norm_exponent), tail)
    tail = jnp.where(lane < LOSS_CODES + 2, tail, 0.0)
    head_row = codes_of(first[...], norm_exponent)
    sub = lax.broadcasted_iota(jnp.int32, (height, half), 0)
    for c in range(chunks):
        value = part[c * share : c * share + height, :]
        bound = jnp.max(jnp.where(sub < share, jnp.abs(value), 0.0), axis=0, keepdims=True)
        exponent = exponent_of(jnp.max(bound, axis=1, keepdims=True))
        last = jnp.where(lane == CHUNK_EXPONENT, exponent, tail)
        codes = jnp.where(
            sub < share, codes_of(value, exponent), jnp.where(sub == share, head_row, last)
        )
        out_ref[c] = codes.astype(jnp.int32).astype(jnp.int16)


def gradient_payload(place, weight, spill, mine, by_mp, by_tower, by_both, chunks, text_width):
    width, half = weight.shape
    height = (width - spill.shape[0]) // chunks + 2
    vmem = pl.BlockSpec(memory_space=pltpu.VMEM)

    def kernel(*refs):
        payload_kernel(text_width, *refs)

    return pl.pallas_call(
        kernel,
        out_shape=jax.ShapeDtypeStruct((chunks, height, half), jnp.int16),
        in_specs=[pl.BlockSpec(memory_space=pltpu.SMEM)] + [vmem] * 6,
        out_specs=vmem,
        scratch_shapes=[
            pltpu.VMEM((width - spill.shape[0] + 8, half), F32),
            pltpu.VMEM((8, width), F32),
            pltpu.VMEM((8, width), F32),
            pltpu.VMEM((1, half), F32),
            pltpu.VMEM((1, half), F32),
        ],
        compiler_params=pltpu.CompilerParams(vmem_limit_bytes=VMEM_LIMIT),
        cost_estimate=pl.CostEstimate(flops=10**7, bytes_accessed=4 * 10**6, transcendentals=0),
        name="gradient_payload",
    )(place, weight, spill, mine, by_mp, by_tower, by_both)


def collect_kernel(got_ref, weight_ref, rest_ref):
    chunks, height, half = got_ref.shape
    sub = lax.broadcasted_iota(jnp.int32, (height, half), 0)
    lane = lax.broadcasted_iota(jnp.int32, (height, half), 1)
    total = jnp.zeros((height, half), F32)
    for c in range(chunks):
        value = got_ref[c].astype(jnp.int32).astype(F32)
        steps = jnp.exp2(value[height - 1 : height, CHUNK_EXPONENT : CHUNK_EXPONENT + BLOCK] - 15.0)

        def step(at):
            return steps[:, at - CHUNK_EXPONENT : at - CHUNK_EXPONENT + 1]

        loss_step = jnp.where(lane == LOSS_CODES, step(LOSS_EXPONENTS), step(LOSS_EXPONENTS + 1))
        last = jnp.where(lane < CHUNK_EXPONENT, step(NORM_EXPONENT), loss_step)
        total += value * jnp.where(
            sub < height - 2,
            step(CHUNK_EXPONENT),
            jnp.where(sub == height - 2, step(NORM_EXPONENT), last),
        )
    weight_ref[...] = total[: height - 2, :]
    rest_ref[...] = total[height - 8 :, :]


def collect(got):
    chunks, height, half = got.shape
    vmem = pl.BlockSpec(memory_space=pltpu.VMEM)
    return pl.pallas_call(
        collect_kernel,
        out_shape=(
            jax.ShapeDtypeStruct((height - 2, half), F32),
            jax.ShapeDtypeStruct((8, half), F32),
        ),
        in_specs=[vmem],
        out_specs=(vmem, vmem),
        compiler_params=pltpu.CompilerParams(vmem_limit_bytes=VMEM_LIMIT),
        cost_estimate=pl.CostEstimate(flops=10**7, bytes_accessed=10**6, transcendentals=0),
        name="collect",
    )(got)


def gather_dp(shard):
    dp_count = lax.axis_size("dp")
    along = min(8, dp_count)
    across = dp_count // along
    rows = shard.shape[0]
    z_groups = [[a * along + z for z in range(along)] for a in range(across)]
    yx_groups = [[a * along + z for a in range(across)] for z in range(along)]
    padded = jnp.pad(shard, ((0, -rows % 8), (0, 0)))
    value = lax.all_to_all(
        jnp.broadcast_to(padded[None], (along, *padded.shape)),
        "dp", 0, 0, tiled=True, axis_index_groups=z_groups,
    )[:, :rows].reshape(along * rows, -1)
    if across > 1:
        value = lax.all_to_all(
            jnp.broadcast_to(value[None], (across, *value.shape)),
            "dp", 0, 0, tiled=True, axis_index_groups=yx_groups,
        ).reshape(dp_count * rows, -1)
    return value


def fixed_scale(exponent):
    return jnp.exp2(exponent - 15.0)


def to_fixed(value, axis):
    top = jnp.maximum(jnp.max(jnp.abs(value), axis=axis, keepdims=True), 1e-30)
    exponent = jnp.ceil(jnp.log2(top))
    codes = jnp.clip(jnp.round(value / fixed_scale(exponent)), -32767.0, 32767.0)
    return codes.astype(jnp.int16), exponent.astype(jnp.int16)


def from_fixed(codes, exponent):
    return codes.astype(F32) * fixed_scale(exponent.astype(F32))


def body(
    image_feats,
    text_feats,
    image_gain,
    image_bias,
    text_gain,
    text_bias,
    image_head,
    text_head,
    running_cov,
    pair_index,
):
    is_image = lax.axis_index("tower") == 0
    mp_index = lax.axis_index("mp")
    rows, image_width = image_feats.shape
    text_width = text_feats.shape[1]
    half = image_head.shape[1]
    width = running_cov.shape[1]
    dp_count = lax.axis_size("dp")
    total_rows = rows * dp_count

    text_head_padded = pad_rows(text_head, image_width)
    head_far = jnp.where(is_image, text_head_padded, image_head)
    head_own = jnp.where(is_image, image_head, text_head_padded)
    near, far = swap_halves(head_far)
    cov_old = flip(running_cov[0], "tower")

    def image_rows():
        return normalize(image_feats, image_gain, image_bias)

    def text_rows():
        standard, normed = normalize(text_feats, text_gain, text_bias)
        return pad_cols(standard, image_width), pad_cols(normed, image_width)

    standard, normed, normed_far = lax.cond(
        is_image,
        lambda: (*image_rows(), text_rows()[1]),
        lambda: (*text_rows(), image_rows()[1]),
    )
    projected = jnp.dot(normed, head_own, preferred_element_type=F32)

    gain_far = jnp.where(is_image, jnp.pad(text_gain, (0, image_width - text_width)), image_gain)
    bias_far = jnp.where(is_image, jnp.pad(text_bias, (0, image_width - text_width)), image_bias)
    head_wide = head_far.astype(F32)
    spread = jnp.sum((gain_far[:, None] * head_wide) ** 2, axis=0)
    middle = jnp.sum(bias_far[:, None] * head_wide, axis=0)
    size = jnp.maximum(spread + middle * middle, 1e-30)
    scale_own = jnp.exp2(-jnp.round(0.5 * jnp.log2(size)))
    scale_other = flip(scale_own, "mp")
    scales = jnp.where(
        mp_index == 0,
        jnp.concatenate([scale_own, scale_other]),
        jnp.concatenate([scale_other, scale_own]),
    )
    own_low = jnp.dot(normed_far, head_far, preferred_element_type=F32).astype(BF16)
    own_low = (own_low.astype(F32) * scale_own[None, :]).astype(BF16)
    mp_scalar = mp_index[None].astype(jnp.int32)
    low_far, cov_codes = covariance_part(
        mp_scalar, normed_far, own_low, near, far, scale_other[None, :], dp_count
    )
    share = PANEL_ROWS // dp_count
    received = lax.all_to_all(cov_codes, "dp", 0, 0, tiled=True)
    cov_shard = jnp.sum(
        from_fixed(received[:, :share], received[:, share : share + 1]), axis=0
    )
    gathered = gather_dp(cov_shard)
    near_panels, far_panels = swap_halves(gathered)
    row_scale, col_scale = scales[:, None], scales[None, :]
    wide, upper = first_factor(mp_scalar, gathered, cov_old, row_scale, col_scale, total_rows)
    near_panels, far_panels, wide, upper = lax.optimization_barrier(
        (near_panels, far_panels, wide, upper)
    )
    inverse_rows, cov_cols = second_factor(
        mp_scalar, gathered, near_panels, far_panels, cov_old, row_scale, col_scale, wide, upper,
        total_rows,
    )
    new_cov = flip(cov_cols, "tower") + 0.5 * lax.dynamic_slice_in_dim(
        running_cov[0], mp_index * half, half, 1
    )

    per_tower = (image_width + text_width) // 2
    grad_low, sums, spill = residual_part(
        is_image[None].astype(jnp.int32), inverse_rows, low_far, projected, pair_index % rows,
        head_own, standard, normed, image_width - per_tower, total_rows,
    )
    spill = flip(spill, "tower")
    across = [(i, 3 - i) for i in range(4)]
    sums_mp, sums_tower = flip(sums, "mp"), flip(sums, "tower")
    sums_both = lax.ppermute(sums, ("tower", "mp"), across)
    weight_grad = contract_rows(normed, grad_low)
    place = lax.axis_index("tower") * 2 + mp_index
    payload = gradient_payload(
        place[None].astype(jnp.int32), weight_grad, spill, sums, sums_mp, sums_tower, sums_both,
        dp_count, text_width,
    )
    got = lax.all_to_all(payload, "dp", 0, 0, tiled=True)
    head_grads, rest = collect(got)
    rest_mp, rest_tower = flip(rest, "mp"), flip(rest, "tower")
    rest_both = lax.ppermute(rest, ("tower", "mp"), across)
    parts = [rest, rest_mp, rest_tower, rest_both]
    quarters = []
    for index in range(4):
        chosen = parts[0]
        for other in range(1, 4):
            chosen = jnp.where(place == index ^ other, parts[other], chosen)
        quarters.append(chosen)
    flat = jnp.concatenate(
        [v for q in quarters for v in (q[6], q[7, : per_tower - half])]
    )
    norm_grads = flat.reshape(2, image_width + text_width)
    losses = rest[7, LOSS_CODES : LOSS_CODES + 2]
    return new_cov[None], head_grads, norm_grads, losses


def solution(mesh):
    return jax.shard_map(
        body,
        mesh=mesh,
        in_specs=(
            P("dp", None),
            P("dp", None),
            P(),
            P(),
            P(),
            P(),
            P(None, "mp"),
            P(None, "mp"),
            P("tower", None, None),
            P("dp"),
        ),
        out_specs=(P("tower", None, "mp"), P(("tower", "dp"), "mp"), P(), P()),
        check_vma=False,
    )
```

```python
import jax
import jax.numpy as jnp
from jax import lax
from jax.experimental import pallas as pl
from jax.experimental.pallas import tpu as pltpu
from jax.sharding import PartitionSpec as P

EPSILON = 1e-05
F32 = jnp.float32
BF16 = jnp.bfloat16
BLOCK = 128
GROUP = 8
PANELS = {
    1: ((0, 0, 8), (1, 1, 7), (2, 2, 3)),
    0: ((2, 5, 3), (3, 3, 5), (4, 4, 4), (5, 5, 3), (6, 6, 2), (7, 7, 1)),
}
PRODUCTS = {
    1: (((0, 2), 0, (0, 1)), ((2, 3), 2, (2,))),
    0: (((2, 4), 3, (0, 1)), ((4, 6), 4, (2, 3)), ((6, 8), 6, (4, 5))),
}
PANEL_ROWS = 18 * BLOCK
WIDE = 2 * BLOCK
MIB = 1024 * 1024


def flip(value, axis):
    return lax.ppermute(value, axis, [(0, 1), (1, 0)])


def swap_halves(first, second):
    dp_count = lax.axis_size("dp")
    x_hi_bit = 8 if dp_count == 64 else 1
    pairs = []
    for dp in range(dp_count):
        for mp in range(2):
            x_hi = (dp // x_hi_bit) % 2
            x = (x_hi * 2 + mp + (-1 if mp == 0 else 1)) % 4
            other = dp - x_hi * x_hi_bit + (x // 2) * x_hi_bit
            pairs.append((dp * 2 + mp, other * 2 + x % 2))
    return flip(first, "mp"), lax.ppermute(second, ("dp", "mp"), pairs)


def normalize(features, gain, bias):
    values = features.astype(F32)
    mean = jnp.mean(values, axis=1, keepdims=True)
    centered = values - mean
    var = jnp.mean(centered * centered, axis=1, keepdims=True)
    standard = centered * lax.rsqrt(var + EPSILON)
    return standard, (standard * gain[None, :] + bias[None, :]).astype(BF16)


def pad_cols(value, width):
    return jnp.pad(value, ((0, 0), (0, width - value.shape[1])))


def pad_rows(value, height):
    return jnp.pad(value, ((0, height - value.shape[0]), (0, 0)))


def contract_rows(a, b):
    return lax.dot_general(a, b, (((0,), (0,)), ((), ())), preferred_element_type=F32)


def precise_dot(a, b, dims):
    return lax.dot_general(
        a, b, (dims, ((), ())), precision=lax.Precision.HIGHEST, preferred_element_type=F32
    )


def tree_sum(terms):
    terms = list(terms)
    while len(terms) > 1:
        terms = [
            terms[a] + terms[a + 1] if a + 1 < len(terms) else terms[a]
            for a in range(0, len(terms), 2)
        ]
    return terms[0]


def factor_block(w_ref, t_ref):
    n = w_ref.shape[0]
    sub = lax.broadcasted_iota(jnp.int32, (GROUP, n), 0)
    lane = lax.broadcasted_iota(jnp.int32, (GROUP, n), 1)
    rows = [w_ref[GROUP * i : GROUP * (i + 1), :] for i in range(n // GROUP)]

    def spread(value):
        return jnp.broadcast_to(value, (GROUP, n))

    for g in range(n // GROUP):
        first = GROUP * g
        inside = (lane >= first) & (lane < first + GROUP)
        cols = [spread(rows[g][:, first + j : first + j + 1]) for j in range(GROUP)]
        e = [[spread(cols[j][i : i + 1, :]) for j in range(i + 1)] for i in range(GROUP)]
        full = jnp.where(inside, jnp.where(lane - first == sub, 1.0, 0.0), rows[g])
        right = [spread(full[k : k + 1, :]) for k in range(GROUP)]
        low = [[None] * GROUP for _ in range(GROUP)]
        roots, upper = [], []
        for j in range(GROUP):
            root = lax.rsqrt(e[j][j])
            roots.append(root)
            upper.append(right[j] * root)
            for i in range(j + 1, GROUP):
                low[i][j] = e[i][j] * root
            for k in range(j + 1, GROUP):
                right[k] = right[k] - low[k][j] * upper[j]
                for i in range(k, GROUP):
                    e[i][k] = e[i][k] - low[i][j] * low[k][j]
        result = upper[-1]
        for j in range(GROUP - 1):
            result = jnp.where(sub == j, upper[j], result)
        t_ref[first : first + GROUP, :] = jnp.where(lane < first + GROUP, result, 0.0)
        for i in range(g + 1, n // GROUP):
            left = []
            for j in range(GROUP):
                entry = spread(rows[i][:, first + j : first + j + 1])
                for k in range(j):
                    entry = entry - left[k] * low[j][k]
                left.append(entry * roots[j])
            rows[i] = jnp.where(inside, 0.0, rows[i]) - tree_sum(
                left[k] * upper[k] for k in range(GROUP)
            )


def covariance_kernel(mp_ref, normed_ref, own_ref, near_ref, far_ref, scale_ref, low_ref, out_ref, panel):
    depth, half = near_ref.shape
    other = jnp.dot(normed_ref[:, :depth], near_ref[...], preferred_element_type=F32)
    other += jnp.dot(normed_ref[:, depth:], far_ref[...], preferred_element_type=F32)
    other = (other.astype(BF16).astype(F32) * scale_ref[...]).astype(BF16)

    def products(index):
        low_ref[:, index * half : (index + 1) * half] = own_ref[...]
        low_ref[:, (1 - index) * half : (2 - index) * half] = other
        offsets = [0]
        for _, _, count in PANELS[index]:
            offsets.append(offsets[-1] + count * BLOCK)
        for (first, last), top, members in PRODUCTS[index]:
            bottom = max(PANELS[index][p][1] + PANELS[index][p][2] for p in members)
            product = contract_rows(
                low_ref[:, top * BLOCK : bottom * BLOCK], low_ref[:, first * BLOCK : last * BLOCK]
            )
            for p in members:
                col, row, count = PANELS[index][p]
                panel[offsets[p] : offsets[p + 1], :] = product[
                    (row - top) * BLOCK : (row - top + count) * BLOCK,
                    (col - first) * BLOCK : (col - first + 1) * BLOCK,
                ]

    for index in range(2):
        pl.when(mp_ref[0] == index)(lambda index=index: products(index))
    chunks, height, _ = out_ref.shape
    share = PANEL_ROWS // chunks
    panel[PANEL_ROWS:, :] = jnp.zeros((panel.shape[0] - PANEL_ROWS, BLOCK), F32)
    sub = lax.broadcasted_iota(jnp.int32, (height, BLOCK), 0)
    for c in range(chunks):
        value = panel[c * share : c * share + height, :]
        top = jnp.max(jnp.where(sub < share, jnp.abs(value), 0.0), axis=0, keepdims=True)
        exponent = jnp.ceil(jnp.log2(jnp.maximum(top, 1e-30)))
        codes = jnp.clip(jnp.round(value * jnp.exp2(15.0 - exponent)), -32767.0, 32767.0)
        codes = jnp.where(sub < share, codes, jnp.where(sub == share, exponent, 0.0))
        out_ref[c] = codes.astype(jnp.int32).astype(jnp.int16)


def covariance_part(mp_index, normed, own, near, far, scale, chunks):
    rows, half = own.shape
    share = PANEL_ROWS // chunks
    height = share + 8 - share % 8
    vmem = pl.BlockSpec(memory_space=pltpu.VMEM)
    return pl.pallas_call(
        covariance_kernel,
        out_shape=(
            jax.ShapeDtypeStruct((rows, 2 * half), BF16),
            jax.ShapeDtypeStruct((chunks, height, BLOCK), jnp.int16),
        ),
        in_specs=[pl.BlockSpec(memory_space=pltpu.SMEM)] + [vmem] * 5,
        out_specs=(vmem, vmem),
        scratch_shapes=[pltpu.VMEM((PANEL_ROWS + 8, BLOCK), F32)],
        compiler_params=pltpu.CompilerParams(vmem_limit_bytes=24 * MIB),
        cost_estimate=pl.CostEstimate(flops=3 * 10**9, bytes_accessed=10**7, transcendentals=0),
        name="covariance_part",
    )(mp_index, normed, own, near, far, scale)


def wide_factor(w_ref, k, blk, t, wide):
    a = pl.ds(pl.multiple_of(k * WIDE, WIDE), BLOCK)
    b = pl.ds(pl.multiple_of(k * WIDE + BLOCK, BLOCK), BLOCK)
    corner = w_ref[b, a]

    def half_step(h, carry):
        @pl.when(h == 0)
        def _():
            blk[...] = w_ref[a, a]

        @pl.when(h == 1)
        def _():
            first = t[...]
            wide[:BLOCK, :BLOCK] = first
            wide[:BLOCK, BLOCK:] = jnp.zeros((BLOCK, BLOCK), F32)
            left = precise_dot(corner, first, ((1,), (1,)))
            wide[BLOCK:, :BLOCK] = precise_dot(left, first, ((1,), (0,)))
            blk[...] = w_ref[b, b] - precise_dot(left, left, ((1,), (1,)))

        factor_block(blk, t)
        return carry

    lax.fori_loop(0, 2, half_step, 0)
    second = t[...]
    wide[BLOCK:, BLOCK:] = second
    wide[BLOCK:, :BLOCK] = -precise_dot(second, wide[BLOCK:, :BLOCK], ((1,), (0,)))


def load_panels(w, old_ref, source, panels, scales, total_rows):
    row_scale, col_scale = scales
    offset = 0
    for col, row, count in panels:
        there = slice(col * BLOCK, (col + 1) * BLOCK)
        for i in range(row, row + count):
            here = slice(i * BLOCK, (i + 1) * BLOCK)
            both = row_scale[here, :] * col_scale[:, there]
            value = 0.5 * old_ref[here, there] * both
            value += (0.5 / total_rows) * source(offset)
            w[here, there] = value
            if i > col:
                w[there, here] = value.T
            offset += BLOCK


def eliminate(k, w, u, small):
    first, last = k * WIDE, (k + 1) * WIDE
    n = w.shape[1]
    if first > 0:
        u[:, :first] = precise_dot(small, w[first:last, :first], ((1,), (0,)))
    u[:, first:last] = small
    if last < n:
        u[:, last:] = precise_dot(small, w[first:last, last:], ((1,), (0,)))


def update_below(k, w, u, small):
    first, last = k * WIDE, (k + 1) * WIDE
    left = precise_dot(w[last:, first:last], small, ((1,), (1,)))
    w[last:, first:last] = jnp.zeros((w.shape[0] - last, WIDE), F32)
    w[last:, :] -= precise_dot(left, u[...], ((1,), (0,)))


def first_kernel(
    total_rows, mp_ref, own_ref, old_hbm, rs_ref, cs_ref, wide_ref, u_ref, w, blk, t, old, sem
):
    @pl.when(mp_ref[0] == 1)
    def _():
        copy = pltpu.make_async_copy(old_hbm.at[:, pl.ds(0, WIDE)], old, sem)
        copy.start()
        copy.wait()

        def own(offset):
            return own_ref[offset : offset + BLOCK, :]

        load_panels(w, old, own, PANELS[1][:2], (rs_ref, cs_ref), total_rows)
        wide_factor(w, 0, blk, t, wide_ref)
        eliminate(0, w, u_ref, wide_ref[...])

    @pl.when(mp_ref[0] == 0)
    def _():
        wide_ref[...] = jnp.zeros(wide_ref.shape, F32)
        u_ref[...] = jnp.zeros(u_ref.shape, F32)


def panel_source(own_ref, near_ref, far_ref):
    split = near_ref.shape[0]

    def own(offset):
        return own_ref[offset : offset + BLOCK, :]

    def other(offset):
        if offset < split:
            return near_ref[offset : offset + BLOCK, :]
        return far_ref[offset - split : offset - split + BLOCK, :]

    return own, other


def columns_kernel(total_rows, mp_ref, own_ref, near_ref, far_ref, rs_ref, cs_ref, cov_ref, rows, cols):
    half = cov_ref.shape[1]
    own, other = panel_source(own_ref, near_ref, far_ref)
    rows[...] = 1.0 / rs_ref[...]
    cols[...] = (0.5 / total_rows) / cs_ref[...]

    def fill(index):
        for source, panels in ((own, PANELS[index]), (other, PANELS[1 - index])):
            offset = 0
            for col, row, count in panels:
                for i in range(row, row + count):
                    value = source(offset)
                    offset += BLOCK
                    for r, c in ((i, col),) if i == col else ((i, col), (col, i)):
                        if c * BLOCK // half != index:
                            continue
                        block = value if r == i else value.T
                        here = slice(r * BLOCK, (r + 1) * BLOCK)
                        there = slice(c * BLOCK, (c + 1) * BLOCK)
                        at = slice(c * BLOCK - index * half, (c + 1) * BLOCK - index * half)
                        cov_ref[here, at] = block * rows[here, :] * cols[:, there]

    for index in range(2):
        pl.when(mp_ref[0] == index)(lambda index=index: fill(index))


def covariance_columns(mp_index, own, near, far, row_scale, col_scale, total_rows):
    n = row_scale.shape[0]
    vmem = pl.BlockSpec(memory_space=pltpu.VMEM)

    def kernel(*refs):
        columns_kernel(total_rows, *refs)

    return pl.pallas_call(
        kernel,
        out_shape=jax.ShapeDtypeStruct((n, n // 2), F32),
        in_specs=[pl.BlockSpec(memory_space=pltpu.SMEM)] + [vmem] * 5,
        out_specs=vmem,
        scratch_shapes=[pltpu.VMEM((n, 1), F32), pltpu.VMEM((1, n), F32)],
        compiler_params=pltpu.CompilerParams(vmem_limit_bytes=16 * MIB),
        cost_estimate=pl.CostEstimate(flops=10**7, bytes_accessed=5 * 10**6, transcendentals=0),
        name="covariance_columns",
    )(mp_index, own, near, far, row_scale, col_scale)


def whiten_kernel(
    total_rows, place_ref, own_ref, near_ref, far_ref, rs_ref, cs_ref, wide_ref, u_ref, row_ref, col_ref,
    old_hbm, low_hbm, proj_hbm, head_hbm, standard_hbm, normed_hbm,
    grad_ref, sums_ref, spill_ref,
    w, blk, t, wide, u, inv, white, old, low, proj, head, standard, normed, sems,
):
    n = w.shape[0]
    half = inv.shape[0]
    steps = n // WIDE
    mp = place_ref[0] % 2
    copies = [
        pltpu.make_async_copy(source, target, sems.at[i])
        for i, (source, target) in enumerate(
            (
                (old_hbm, old),
                (low_hbm, low),
                (proj_hbm, proj),
                (head_hbm, head),
                (standard_hbm, standard),
                (normed_hbm, normed),
            )
        )
    ]
    for copy in copies:
        copy.start()
    copies[0].wait()
    own, other = panel_source(own_ref, near_ref, far_ref)
    for index in range(2):
        @pl.when(mp == index)
        def _():
            load_panels(w, old, own, PANELS[index], (rs_ref, cs_ref), total_rows)
            load_panels(w, old, other, PANELS[1 - index], (rs_ref, cs_ref), total_rows)

    wide[...] = wide_ref[...]
    u[...] = u_ref[...]

    def step(k, carry):
        @pl.when((k > 0) | (mp == 0))
        def _():
            wide_factor(w, k, blk, t, wide)

        def whole_step(index):
            small = wide[...]
            if index > 0:
                eliminate(index, w, u, small)
            else:
                @pl.when(mp == 0)
                def _():
                    eliminate(index, w, u, small)

            @pl.when(mp == index * WIDE // half)
            def _():
                here = slice(index * WIDE % half, index * WIDE % half + WIDE)
                last = (index + 1) * WIDE
                inv[here, :last] = u[:, :last]
                if last < n:
                    inv[here, last:] = jnp.zeros((WIDE, n - last), F32)

            if index + 1 < steps:
                update_below(index, w, u, small)

        for index in range(steps):
            pl.when(k == index)(lambda index=index: whole_step(index))
        return carry

    lax.fori_loop(0, jnp.where(mp == 0, half // WIDE, steps), step, 0)
    for copy in copies[1:]:
        copy.wait()
    residual_kernel(
        total_rows, place_ref[0] < 2, inv, low, proj, row_ref, col_ref, head, standard, normed,
        grad_ref, sums_ref, spill_ref, white,
    )


def first_factor(mp_index, own, cov_old, row_scale, col_scale, total_rows):
    n = cov_old.shape[0]
    vmem = pl.BlockSpec(memory_space=pltpu.VMEM)

    def kernel(*refs):
        first_kernel(total_rows, *refs)

    return pl.pallas_call(
        kernel,
        out_shape=(
            jax.ShapeDtypeStruct((WIDE, WIDE), F32),
            jax.ShapeDtypeStruct((WIDE, n), F32),
        ),
        in_specs=[
            pl.BlockSpec(memory_space=pltpu.SMEM),
            vmem,
            pl.BlockSpec(memory_space=pl.ANY),
            vmem,
            vmem,
        ],
        out_specs=(vmem, vmem),
        scratch_shapes=[
            pltpu.VMEM((n, n), F32),
            pltpu.VMEM((BLOCK, BLOCK), F32),
            pltpu.VMEM((BLOCK, BLOCK), F32),
            pltpu.VMEM((n, WIDE), F32),
            pltpu.SemaphoreType.DMA,
        ],
        compiler_params=pltpu.CompilerParams(vmem_limit_bytes=20 * MIB),
        cost_estimate=pl.CostEstimate(flops=15 * 10**9, bytes_accessed=10**7, transcendentals=0),
        name="first_factor",
    )(mp_index, own, cov_old, row_scale, col_scale)


def residual_kernel(
    total_rows, is_image, inv_ref, low_ref, proj_ref, row_ref, col_ref, head_ref, standard_ref,
    normed_ref, grad_ref, sums_ref, spill_ref, white,
):
    rows, half = proj_ref.shape
    width = low_ref.shape[1]
    left = inv_ref[...]
    high = left.astype(BF16)
    left = left - high.astype(F32)
    middle = left.astype(BF16)
    small = (left - middle.astype(F32)).astype(BF16)
    dims = (((1,), (1,)), ((), ()))
    tile = 256
    for r in range(0, rows, tile):
        low = low_ref[r : r + tile, :]
        value = lax.dot_general(low, small, dims, preferred_element_type=F32)
        value += lax.dot_general(low, middle, dims, preferred_element_type=F32)
        value += lax.dot_general(low, high, dims, preferred_element_type=F32)
        white[r : r + tile, :] = value.astype(BF16)
    lane = lax.broadcasted_iota(jnp.int32, (tile, rows), 1)
    sub = lax.broadcasted_iota(jnp.int32, (tile, rows), 0)
    wanted = jnp.where(is_image, 1, 0)
    gain = jnp.zeros((1, width), F32)
    shift = jnp.zeros((1, width), F32)
    total = jnp.zeros((1, half), F32)
    for r in range(0, rows, tile):
        from_image = jnp.where(col_ref[r : r + tile, :] == lane, wanted, 0)
        from_text = jnp.where(row_ref[...] == sub + r, 1 - wanted, 0)
        chosen = (from_image + from_text).astype(F32).astype(BF16)
        targets = jnp.dot(chosen, white[...], preferred_element_type=F32)
        residual = proj_ref[r : r + tile, :] - targets
        total += jnp.sum(residual * residual, axis=0, keepdims=True)
        grad = (residual * (1.0 / width)).astype(BF16)
        grad_ref[r : r + tile, :] = grad
        dnormed = lax.dot_general(grad, head_ref[...], dims, preferred_element_type=F32)
        gain += jnp.sum(standard_ref[r : r + tile, :] * dnormed, axis=0, keepdims=True)
        shift += jnp.sum(dnormed, axis=0, keepdims=True)
    sums_ref[0:1, :] = gain
    sums_ref[1:2, :] = shift
    loss_value = jnp.sum(total, axis=1, keepdims=True) / (2.0 * total_rows * width)
    sums_ref[2:8, :] = jnp.broadcast_to(loss_value, (6, width))
    kept = width - spill_ref.shape[0]
    spill_ref[...] = contract_rows(normed_ref[:, kept:], grad_ref[...])


def whitened_residual(
    place, own, near, far, row_scale, col_scale, wide, upper, pairs,
    cov_old, low, projected, head, standard, normed, spilled, total_rows,
):
    rows, half = projected.shape
    n = cov_old.shape[0]
    vmem = pl.BlockSpec(memory_space=pltpu.VMEM)
    anywhere = pl.BlockSpec(memory_space=pl.ANY)

    def kernel(*refs):
        whiten_kernel(total_rows, *refs)

    return pl.pallas_call(
        kernel,
        out_shape=(
            jax.ShapeDtypeStruct((rows, half), BF16),
            jax.ShapeDtypeStruct((8, n), F32),
            jax.ShapeDtypeStruct((spilled, half), F32),
        ),
        in_specs=[pl.BlockSpec(memory_space=pltpu.SMEM)] + [vmem] * 9 + [anywhere] * 6,
        out_specs=(vmem, vmem, vmem),
        scratch_shapes=[
            pltpu.VMEM((n, n), F32),
            pltpu.VMEM((BLOCK, BLOCK), F32),
            pltpu.VMEM((BLOCK, BLOCK), F32),
            pltpu.VMEM((WIDE, WIDE), F32),
            pltpu.VMEM((WIDE, n), F32),
            pltpu.VMEM((half, n), F32),
            pltpu.VMEM((rows, half), BF16),
            pltpu.VMEM((n, n), F32),
            pltpu.VMEM((rows, n), BF16),
            pltpu.VMEM((rows, half), F32),
            pltpu.VMEM(head.shape, BF16),
            pltpu.VMEM(standard.shape, F32),
            pltpu.VMEM(normed.shape, BF16),
            pltpu.SemaphoreType.DMA((6,)),
        ],
        compiler_params=pltpu.CompilerParams(vmem_limit_bytes=48 * MIB),
        cost_estimate=pl.CostEstimate(flops=60 * 10**9, bytes_accessed=2 * 10**7, transcendentals=0),
        name="whitened_residual",
    )(
        place, own, near, far, row_scale, col_scale, wide, upper, pairs[None, :], pairs[:, None],
        cov_old, low, projected, head, standard, normed,
    )


CHUNK_EXPONENT, NORM_EXPONENT, LOSS_EXPONENTS, LOSS_CODES = 384, 385, 386, 388


def exponent_of(value):
    return jnp.ceil(jnp.log2(jnp.maximum(jnp.abs(value), 1e-30)))


def codes_of(value, exponent):
    return jnp.clip(jnp.round(value * jnp.exp2(15.0 - exponent)), -32767.0, 32767.0)


def payload_kernel(
    text_width, place_ref, weight_ref, spill_ref, mine_ref, mp_ref, tower_ref, both_ref,
    out_ref, part, image, text, first, second,
):
    chunks, height, half = out_ref.shape
    spilled = spill_ref.shape[0]
    kept = weight_ref.shape[0] - spilled
    share = kept // chunks
    width = mine_ref.shape[1]
    place = place_ref[0]
    mine = mine_ref[...] + mp_ref[...]
    theirs = tower_ref[...] + both_ref[...]

    @pl.when(place < 2)
    def _():
        part[:kept, :] = weight_ref[:kept, :]
        image[...] = mine
        text[...] = theirs

    @pl.when(place >= 2)
    def _():
        part[:spilled, :] = spill_ref[...]
        part[spilled:kept, :] = weight_ref[: kept - spilled, :]
        image[...] = theirs
        text[...] = mine

    part[kept:, :] = jnp.zeros((part.shape[0] - kept, half), F32)
    second[...] = jnp.zeros(second.shape, F32)
    quarter = (width + text_width) // 2
    for index in range(4):
        @pl.when(place == index)
        def _():
            row = slice(index // 2, index // 2 + 1)
            pieces = [(image, c) for c in range(0, width, BLOCK)]
            pieces += [(text, c) for c in range(0, text_width, BLOCK)]
            start = (index % 2) * quarter // BLOCK
            for i, (ref, c) in enumerate(pieces[start : start + quarter // BLOCK]):
                if i * BLOCK < half:
                    first[:, i * BLOCK : (i + 1) * BLOCK] = ref[row, c : c + BLOCK]
                else:
                    at = i * BLOCK - half
                    second[:, at : at + BLOCK] = ref[row, c : c + BLOCK]

    lane = lax.broadcasted_iota(jnp.int32, (1, half), 1)
    top = jnp.maximum(
        jnp.max(jnp.abs(first[...]), axis=1, keepdims=True),
        jnp.max(jnp.abs(second[...]), axis=1, keepdims=True),
    )
    norm_exponent = exponent_of(top)
    loss = jnp.where(lane % 2 == 0, image[2:3, :half], text[2:3, :half])
    loss_exponent = exponent_of(loss)
    tail = jnp.where(lane < LOSS_CODES, loss_exponent, codes_of(loss, loss_exponent))
    tail = jnp.where(lane == NORM_EXPONENT, norm_exponent, tail)
    tail = jnp.where(lane < CHUNK_EXPONENT, codes_of(second[...], norm_exponent), tail)
    tail = jnp.where(lane < LOSS_CODES + 2, tail, 0.0)
    head_row = codes_of(first[...], norm_exponent)
    sub = lax.broadcasted_iota(jnp.int32, (height, half), 0)
    for c in range(chunks):
        value = part[c * share : c * share + height, :]
        bound = jnp.max(jnp.where(sub < share, jnp.abs(value), 0.0), axis=0, keepdims=True)
        exponent = exponent_of(jnp.max(bound, axis=1, keepdims=True))
        last = jnp.where(lane == CHUNK_EXPONENT, exponent, tail)
        codes = jnp.where(
            sub < share, codes_of(value, exponent), jnp.where(sub == share, head_row, last)
        )
        out_ref[c] = codes.astype(jnp.int32).astype(jnp.int16)


def gradient_payload(place, weight, spill, mine, by_mp, by_tower, by_both, chunks, text_width):
    width, half = weight.shape
    height = (width - spill.shape[0]) // chunks + 2
    vmem = pl.BlockSpec(memory_space=pltpu.VMEM)

    def kernel(*refs):
        payload_kernel(text_width, *refs)

    return pl.pallas_call(
        kernel,
        out_shape=jax.ShapeDtypeStruct((chunks, height, half), jnp.int16),
        in_specs=[pl.BlockSpec(memory_space=pltpu.SMEM)] + [vmem] * 6,
        out_specs=vmem,
        scratch_shapes=[
            pltpu.VMEM((width - spill.shape[0] + 8, half), F32),
            pltpu.VMEM((8, width), F32),
            pltpu.VMEM((8, width), F32),
            pltpu.VMEM((1, half), F32),
            pltpu.VMEM((1, half), F32),
        ],
        compiler_params=pltpu.CompilerParams(vmem_limit_bytes=20 * MIB),
        cost_estimate=pl.CostEstimate(flops=10**7, bytes_accessed=4 * 10**6, transcendentals=0),
        name="gradient_payload",
    )(place, weight, spill, mine, by_mp, by_tower, by_both)


def collect_kernel(got_ref, weight_ref, rest_ref):
    chunks, height, half = got_ref.shape
    sub = lax.broadcasted_iota(jnp.int32, (height, half), 0)
    lane = lax.broadcasted_iota(jnp.int32, (height, half), 1)
    total = jnp.zeros((height, half), F32)
    for c in range(chunks):
        value = got_ref[c].astype(jnp.int32).astype(F32)
        steps = jnp.exp2(value[height - 1 : height, CHUNK_EXPONENT : CHUNK_EXPONENT + BLOCK] - 15.0)

        def step(at):
            return steps[:, at - CHUNK_EXPONENT : at - CHUNK_EXPONENT + 1]

        loss_step = jnp.where(lane == LOSS_CODES, step(LOSS_EXPONENTS), step(LOSS_EXPONENTS + 1))
        last = jnp.where(lane < CHUNK_EXPONENT, step(NORM_EXPONENT), loss_step)
        total += value * jnp.where(
            sub < height - 2,
            step(CHUNK_EXPONENT),
            jnp.where(sub == height - 2, step(NORM_EXPONENT), last),
        )
    weight_ref[...] = total[: height - 2, :]
    rest_ref[...] = total[height - 8 :, :]


def collect(got):
    chunks, height, half = got.shape
    vmem = pl.BlockSpec(memory_space=pltpu.VMEM)
    return pl.pallas_call(
        collect_kernel,
        out_shape=(
            jax.ShapeDtypeStruct((height - 2, half), F32),
            jax.ShapeDtypeStruct((8, half), F32),
        ),
        in_specs=[vmem],
        out_specs=(vmem, vmem),
        compiler_params=pltpu.CompilerParams(vmem_limit_bytes=12 * MIB),
        cost_estimate=pl.CostEstimate(flops=10**7, bytes_accessed=10**6, transcendentals=0),
        name="collect",
    )(got)


def gather_dp(shard):
    dp_count = lax.axis_size("dp")
    along = min(8, dp_count)
    across = dp_count // along
    rows = shard.shape[0]
    z_groups = [[a * along + z for z in range(along)] for a in range(across)]
    yx_groups = [[a * along + z for a in range(across)] for z in range(along)]
    padded = jnp.pad(shard, ((0, -rows % 8), (0, 0)))
    value = lax.all_to_all(
        jnp.broadcast_to(padded[None], (along, *padded.shape)),
        "dp", 0, 0, tiled=True, axis_index_groups=z_groups,
    )[:, :rows].reshape(along * rows, -1)
    if across > 1:
        value = lax.all_to_all(
            jnp.broadcast_to(value[None], (across, *value.shape)),
            "dp", 0, 0, tiled=True, axis_index_groups=yx_groups,
        ).reshape(dp_count * rows, -1)
    return value


def fixed_scale(exponent):
    return jnp.exp2(exponent - 15.0)


def to_fixed(value, axis):
    top = jnp.maximum(jnp.max(jnp.abs(value), axis=axis, keepdims=True), 1e-30)
    exponent = jnp.ceil(jnp.log2(top))
    codes = jnp.clip(jnp.round(value / fixed_scale(exponent)), -32767.0, 32767.0)
    return codes.astype(jnp.int16), exponent.astype(jnp.int16)


def from_fixed(codes, exponent):
    return codes.astype(F32) * fixed_scale(exponent.astype(F32))


def body(
    image_feats,
    text_feats,
    image_gain,
    image_bias,
    text_gain,
    text_bias,
    image_head,
    text_head,
    running_cov,
    pair_index,
):
    is_image = lax.axis_index("tower") == 0
    mp_index = lax.axis_index("mp")
    rows, image_width = image_feats.shape
    text_width = text_feats.shape[1]
    half = image_head.shape[1]
    width = running_cov.shape[1]
    dp_count = lax.axis_size("dp")
    total_rows = rows * dp_count

    depth = image_width // 2
    text_head_padded = pad_rows(text_head, image_width)
    near, far = swap_halves(
        jnp.where(is_image, text_head[:depth], image_head[:depth]),
        jnp.where(is_image, text_head_padded[depth:], image_head[depth:]),
    )
    cov_old = flip(running_cov[0], "tower")

    def text_rows(feats):
        standard, normed = normalize(feats, text_gain, text_bias)
        return pad_cols(standard, image_width), pad_cols(normed, image_width)

    normed_far = lax.cond(
        is_image,
        lambda: text_rows(text_feats)[1],
        lambda: normalize(image_feats, image_gain, image_bias)[1],
    )
    head_far = jnp.where(is_image, text_head_padded, image_head)

    gain_far = jnp.where(is_image, jnp.pad(text_gain, (0, image_width - text_width)), image_gain)
    bias_far = jnp.where(is_image, jnp.pad(text_bias, (0, image_width - text_width)), image_bias)
    head_wide = head_far.astype(F32)
    spread = jnp.sum((gain_far[:, None] * head_wide) ** 2, axis=0)
    middle = jnp.sum(bias_far[:, None] * head_wide, axis=0)
    size = jnp.maximum(spread + middle * middle, 1e-30)
    scale_own = jnp.exp2(-jnp.clip(jnp.round(0.5 * jnp.log2(size)), -20.0, 20.0))
    scale_other = flip(scale_own, "mp")
    scales = jnp.where(
        mp_index == 0,
        jnp.concatenate([scale_own, scale_other]),
        jnp.concatenate([scale_other, scale_own]),
    )
    own_low = jnp.dot(normed_far, head_far, preferred_element_type=F32).astype(BF16)
    own_low = (own_low.astype(F32) * scale_own[None, :]).astype(BF16)
    mp_scalar = mp_index[None].astype(jnp.int32)
    low_far, cov_codes = covariance_part(
        mp_scalar, normed_far, own_low, near, far, scale_other[None, :], dp_count
    )
    cov_codes, image_later, text_later = lax.optimization_barrier(
        (cov_codes, image_feats, text_feats)
    )
    standard, normed = lax.cond(
        is_image,
        lambda: normalize(image_later, image_gain, image_bias),
        lambda: text_rows(text_later),
    )
    head_own = jnp.where(is_image, image_head, text_head_padded)
    projected = jnp.dot(normed, head_own, preferred_element_type=F32)
    share = PANEL_ROWS // dp_count
    received = lax.all_to_all(cov_codes, "dp", 0, 0, tiled=True)
    cov_shard = jnp.sum(
        from_fixed(received[:, :share], received[:, share : share + 1]), axis=0
    )
    gathered = gather_dp(cov_shard)
    near_panels, far_panels = swap_halves(
        gathered[: PANEL_ROWS // 2], gathered[PANEL_ROWS // 2 :]
    )
    row_scale, col_scale = scales[:, None], scales[None, :]
    wide, upper = first_factor(mp_scalar, gathered, cov_old, row_scale, col_scale, total_rows)
    near_panels, far_panels, wide, upper = lax.optimization_barrier(
        (near_panels, far_panels, wide, upper)
    )
    per_tower = (image_width + text_width) // 2
    place = lax.axis_index("tower") * 2 + mp_index
    place_scalar = place[None].astype(jnp.int32)
    grad_low, sums, spill = whitened_residual(
        place_scalar, gathered, near_panels, far_panels, row_scale, col_scale, wide, upper,
        pair_index % rows, cov_old, low_far, projected, head_own, standard, normed,
        image_width - per_tower, total_rows,
    )
    spill = flip(spill, "tower")
    across = [(i, 3 - i) for i in range(4)]
    sums_mp, sums_tower = flip(sums, "mp"), flip(sums, "tower")
    sums_both = lax.ppermute(sums, ("tower", "mp"), across)
    weight_grad = contract_rows(normed, grad_low)
    payload = gradient_payload(
        place_scalar, weight_grad, spill, sums, sums_mp, sums_tower, sums_both,
        dp_count, text_width,
    )
    payload, own_panels, near_panels, far_panels = lax.optimization_barrier(
        (payload, gathered, near_panels, far_panels)
    )
    got = lax.all_to_all(payload, "dp", 0, 0, tiled=True)
    cov_cols = covariance_columns(
        mp_scalar, own_panels, near_panels, far_panels, row_scale, col_scale, total_rows
    )
    new_cov = flip(cov_cols, "tower") + 0.5 * lax.dynamic_slice_in_dim(
        running_cov[0], mp_index * half, half, 1
    )
    head_grads, rest = collect(got)
    rest_mp, rest_tower = flip(rest, "mp"), flip(rest, "tower")
    rest_both = lax.ppermute(rest, ("tower", "mp"), across)
    parts = [rest, rest_mp, rest_tower, rest_both]
    quarters = []
    for index in range(4):
        chosen = parts[0]
        for other in range(1, 4):
            chosen = jnp.where(place == index ^ other, parts[other], chosen)
        quarters.append(chosen)
    flat = jnp.concatenate(
        [v for q in quarters for v in (q[6], q[7, : per_tower - half])]
    )
    norm_grads = flat.reshape(2, image_width + text_width)
    losses = rest[7, LOSS_CODES : LOSS_CODES + 2]
    return new_cov[None], head_grads, norm_grads, losses


def solution(mesh):
    return jax.shard_map(
        body,
        mesh=mesh,
        in_specs=(
            P("dp", None),
            P("dp", None),
            P(),
            P(),
            P(),
            P(),
            P(None, "mp"),
            P(None, "mp"),
            P("tower", None, None),
            P("dp"),
        ),
        out_specs=(P("tower", None, "mp"), P(("tower", "dp"), "mp"), P(), P()),
        check_vma=False,
    )
```

```python
import jax
import jax.numpy as jnp
from jax import lax
from jax.experimental import pallas as pl
from jax.experimental.pallas import tpu as pltpu
from jax.sharding import PartitionSpec as P

EPSILON = 1e-05
F32 = jnp.float32
BF16 = jnp.bfloat16
BLOCK = 128
GROUP = 8
PANELS = {
    1: ((0, 0, 8), (1, 1, 7), (2, 2, 3)),
    0: ((2, 5, 3), (3, 3, 5), (4, 4, 4), (5, 5, 3), (6, 6, 2), (7, 7, 1)),
}
PRODUCTS = {
    1: (((0, 2), 0, (0, 1)), ((2, 3), 2, (2,))),
    0: (((2, 4), 3, (0, 1)), ((4, 6), 4, (2, 3)), ((6, 8), 6, (4, 5))),
}
PANEL_ROWS = 18 * BLOCK
WIDE = 2 * BLOCK
MIB = 1024 * 1024


def flip(value, axis):
    return lax.ppermute(value, axis, [(0, 1), (1, 0)])


def swap_halves(first, second):
    dp_count = lax.axis_size("dp")
    x_hi_bit = 8 if dp_count == 64 else 1
    pairs = []
    for dp in range(dp_count):
        for mp in range(2):
            x_hi = (dp // x_hi_bit) % 2
            x = (x_hi * 2 + mp + (-1 if mp == 0 else 1)) % 4
            other = dp - x_hi * x_hi_bit + (x // 2) * x_hi_bit
            pairs.append((dp * 2 + mp, other * 2 + x % 2))
    return flip(first, "mp"), lax.ppermute(second, ("dp", "mp"), pairs)


def normalize(features, gain, bias):
    values = features.astype(F32)
    mean = jnp.mean(values, axis=1, keepdims=True)
    centered = values - mean
    var = jnp.mean(centered * centered, axis=1, keepdims=True)
    standard = centered * lax.rsqrt(var + EPSILON)
    return standard, (standard * gain[None, :] + bias[None, :]).astype(BF16)


def pad_cols(value, width):
    return jnp.pad(value, ((0, 0), (0, width - value.shape[1])))


def pad_rows(value, height):
    return jnp.pad(value, ((0, height - value.shape[0]), (0, 0)))


def contract_rows(a, b):
    return lax.dot_general(a, b, (((0,), (0,)), ((), ())), preferred_element_type=F32)


def precise_dot(a, b, dims):
    return lax.dot_general(
        a, b, (dims, ((), ())), precision=lax.Precision.HIGHEST, preferred_element_type=F32
    )


def tree_sum(terms):
    terms = list(terms)
    while len(terms) > 1:
        terms = [
            terms[a] + terms[a + 1] if a + 1 < len(terms) else terms[a]
            for a in range(0, len(terms), 2)
        ]
    return terms[0]


def factor_block(w_ref, t_ref):
    n = w_ref.shape[0]
    sub = lax.broadcasted_iota(jnp.int32, (GROUP, n), 0)
    lane = lax.broadcasted_iota(jnp.int32, (GROUP, n), 1)
    rows = [w_ref[GROUP * i : GROUP * (i + 1), :] for i in range(n // GROUP)]

    def spread(value):
        return jnp.broadcast_to(value, (GROUP, n))

    for g in range(n // GROUP):
        first = GROUP * g
        inside = (lane >= first) & (lane < first + GROUP)
        cols = [spread(rows[g][:, first + j : first + j + 1]) for j in range(GROUP)]
        e = [[spread(cols[j][i : i + 1, :]) for j in range(i + 1)] for i in range(GROUP)]
        full = jnp.where(inside, jnp.where(lane - first == sub, 1.0, 0.0), rows[g])
        right = [spread(full[k : k + 1, :]) for k in range(GROUP)]
        low = [[None] * GROUP for _ in range(GROUP)]
        roots, upper = [], []
        for j in range(GROUP):
            root = lax.rsqrt(e[j][j])
            roots.append(root)
            upper.append(right[j] * root)
            for i in range(j + 1, GROUP):
                low[i][j] = e[i][j] * root
            for k in range(j + 1, GROUP):
                right[k] = right[k] - low[k][j] * upper[j]
                for i in range(k, GROUP):
                    e[i][k] = e[i][k] - low[i][j] * low[k][j]
        result = upper[-1]
        for j in range(GROUP - 1):
            result = jnp.where(sub == j, upper[j], result)
        t_ref[first : first + GROUP, :] = jnp.where(lane < first + GROUP, result, 0.0)
        for i in range(g + 1, n // GROUP):
            left = []
            for j in range(GROUP):
                entry = spread(rows[i][:, first + j : first + j + 1])
                for k in range(j):
                    entry = entry - left[k] * low[j][k]
                left.append(entry * roots[j])
            rows[i] = jnp.where(inside, 0.0, rows[i]) - tree_sum(
                left[k] * upper[k] for k in range(GROUP)
            )


def covariance_kernel(mp_ref, normed_ref, own_ref, near_ref, far_ref, scale_ref, low_ref, out_ref, panel):
    depth, half = near_ref.shape
    other = jnp.dot(normed_ref[:, :depth], near_ref[...], preferred_element_type=F32)
    other += jnp.dot(normed_ref[:, depth:], far_ref[...], preferred_element_type=F32)
    other = (other.astype(BF16).astype(F32) * scale_ref[...]).astype(BF16)

    def products(index):
        low_ref[:, index * half : (index + 1) * half] = own_ref[...]
        low_ref[:, (1 - index) * half : (2 - index) * half] = other
        offsets = [0]
        for _, _, count in PANELS[index]:
            offsets.append(offsets[-1] + count * BLOCK)
        for (first, last), top, members in PRODUCTS[index]:
            bottom = max(PANELS[index][p][1] + PANELS[index][p][2] for p in members)
            product = contract_rows(
                low_ref[:, top * BLOCK : bottom * BLOCK], low_ref[:, first * BLOCK : last * BLOCK]
            )
            for p in members:
                col, row, count = PANELS[index][p]
                panel[offsets[p] : offsets[p + 1], :] = product[
                    (row - top) * BLOCK : (row - top + count) * BLOCK,
                    (col - first) * BLOCK : (col - first + 1) * BLOCK,
                ]

    for index in range(2):
        pl.when(mp_ref[0] == index)(lambda index=index: products(index))
    chunks, height, _ = out_ref.shape
    share = PANEL_ROWS // chunks
    panel[PANEL_ROWS:, :] = jnp.zeros((panel.shape[0] - PANEL_ROWS, BLOCK), F32)
    sub = lax.broadcasted_iota(jnp.int32, (height, BLOCK), 0)
    for c in range(chunks):
        value = panel[c * share : c * share + height, :]
        top = jnp.max(jnp.where(sub < share, jnp.abs(value), 0.0), axis=0, keepdims=True)
        exponent = jnp.ceil(jnp.log2(jnp.maximum(top, 1e-30)))
        codes = jnp.clip(jnp.round(value * jnp.exp2(15.0 - exponent)), -32767.0, 32767.0)
        codes = jnp.where(sub < share, codes, jnp.where(sub == share, exponent, 0.0))
        out_ref[c] = codes.astype(jnp.int32).astype(jnp.int16)


def covariance_part(mp_index, normed, own, near, far, scale, chunks):
    rows, half = own.shape
    share = PANEL_ROWS // chunks
    height = share + 8 - share % 8
    vmem = pl.BlockSpec(memory_space=pltpu.VMEM)
    return pl.pallas_call(
        covariance_kernel,
        out_shape=(
            jax.ShapeDtypeStruct((rows, 2 * half), BF16),
            jax.ShapeDtypeStruct((chunks, height, BLOCK), jnp.int16),
        ),
        in_specs=[pl.BlockSpec(memory_space=pltpu.SMEM)] + [vmem] * 5,
        out_specs=(vmem, vmem),
        scratch_shapes=[pltpu.VMEM((PANEL_ROWS + 8, BLOCK), F32)],
        compiler_params=pltpu.CompilerParams(vmem_limit_bytes=24 * MIB),
        cost_estimate=pl.CostEstimate(flops=3 * 10**9, bytes_accessed=10**7, transcendentals=0),
        name="covariance_part",
    )(mp_index, normed, own, near, far, scale)


def wide_factor(w_ref, k, blk, t, wide):
    a = pl.ds(pl.multiple_of(k * WIDE, WIDE), BLOCK)
    b = pl.ds(pl.multiple_of(k * WIDE + BLOCK, BLOCK), BLOCK)
    corner = w_ref[b, a]

    def half_step(h, carry):
        @pl.when(h == 0)
        def _():
            blk[...] = w_ref[a, a]

        @pl.when(h == 1)
        def _():
            first = t[...]
            wide[:BLOCK, :BLOCK] = first
            wide[:BLOCK, BLOCK:] = jnp.zeros((BLOCK, BLOCK), F32)
            left = precise_dot(corner, first, ((1,), (1,)))
            wide[BLOCK:, :BLOCK] = precise_dot(left, first, ((1,), (0,)))
            blk[...] = w_ref[b, b] - precise_dot(left, left, ((1,), (1,)))

        factor_block(blk, t)
        return carry

    lax.fori_loop(0, 2, half_step, 0)
    second = t[...]
    wide[BLOCK:, BLOCK:] = second
    wide[BLOCK:, :BLOCK] = -precise_dot(second, wide[BLOCK:, :BLOCK], ((1,), (0,)))


def load_panels(w, old_ref, source, panels, scales, total_rows):
    row_scale, col_scale = scales
    offset = 0
    for col, row, count in panels:
        there = slice(col * BLOCK, (col + 1) * BLOCK)
        for i in range(row, row + count):
            here = slice(i * BLOCK, (i + 1) * BLOCK)
            both = row_scale[here, :] * col_scale[:, there]
            value = 0.5 * old_ref[here, there] * both
            value += (0.5 / total_rows) * source(offset)
            w[here, there] = value
            if i > col:
                w[there, here] = value.T
            offset += BLOCK


def eliminate(k, w, u, small):
    first, last = k * WIDE, (k + 1) * WIDE
    n = w.shape[1]
    if first > 0:
        u[:, :first] = precise_dot(small, w[first:last, :first], ((1,), (0,)))
    u[:, first:last] = small
    if last < n:
        u[:, last:] = precise_dot(small, w[first:last, last:], ((1,), (0,)))


def update_below(k, w, u, small):
    first, last = k * WIDE, (k + 1) * WIDE
    left = precise_dot(w[last:, first:last], small, ((1,), (1,)))
    w[last:, first:last] = jnp.zeros((w.shape[0] - last, WIDE), F32)
    w[last:, :] -= precise_dot(left, u[...], ((1,), (0,)))


def first_kernel(
    total_rows, mp_ref, own_ref, old_hbm, rs_ref, cs_ref, wide_ref, u_ref, w, blk, t, old, sem
):
    @pl.when(mp_ref[0] == 1)
    def _():
        copy = pltpu.make_async_copy(old_hbm.at[:, pl.ds(0, WIDE)], old, sem)
        copy.start()
        copy.wait()

        def own(offset):
            return own_ref[offset : offset + BLOCK, :]

        load_panels(w, old, own, PANELS[1][:2], (rs_ref, cs_ref), total_rows)
        wide_factor(w, 0, blk, t, wide_ref)
        eliminate(0, w, u_ref, wide_ref[...])

    @pl.when(mp_ref[0] == 0)
    def _():
        wide_ref[...] = jnp.zeros(wide_ref.shape, F32)
        u_ref[...] = jnp.zeros(u_ref.shape, F32)


def panel_source(own_ref, near_ref, far_ref):
    split = near_ref.shape[0]

    def own(offset):
        return own_ref[offset : offset + BLOCK, :]

    def other(offset):
        if offset < split:
            return near_ref[offset : offset + BLOCK, :]
        return far_ref[offset - split : offset - split + BLOCK, :]

    return own, other


def columns_kernel(total_rows, mp_ref, own_ref, near_ref, far_ref, rs_ref, cs_ref, cov_ref, rows, cols):
    half = cov_ref.shape[1]
    own, other = panel_source(own_ref, near_ref, far_ref)
    rows[...] = 1.0 / rs_ref[...]
    cols[...] = (0.5 / total_rows) / cs_ref[...]

    def fill(index):
        for source, panels in ((own, PANELS[index]), (other, PANELS[1 - index])):
            offset = 0
            for col, row, count in panels:
                for i in range(row, row + count):
                    value = source(offset)
                    offset += BLOCK
                    for r, c in ((i, col),) if i == col else ((i, col), (col, i)):
                        if c * BLOCK // half != index:
                            continue
                        block = value if r == i else value.T
                        here = slice(r * BLOCK, (r + 1) * BLOCK)
                        there = slice(c * BLOCK, (c + 1) * BLOCK)
                        at = slice(c * BLOCK - index * half, (c + 1) * BLOCK - index * half)
                        cov_ref[here, at] = block * rows[here, :] * cols[:, there]

    for index in range(2):
        pl.when(mp_ref[0] == index)(lambda index=index: fill(index))


def covariance_columns(mp_index, own, near, far, row_scale, col_scale, total_rows):
    n = row_scale.shape[0]
    vmem = pl.BlockSpec(memory_space=pltpu.VMEM)

    def kernel(*refs):
        columns_kernel(total_rows, *refs)

    return pl.pallas_call(
        kernel,
        out_shape=jax.ShapeDtypeStruct((n, n // 2), F32),
        in_specs=[pl.BlockSpec(memory_space=pltpu.SMEM)] + [vmem] * 5,
        out_specs=vmem,
        scratch_shapes=[pltpu.VMEM((n, 1), F32), pltpu.VMEM((1, n), F32)],
        compiler_params=pltpu.CompilerParams(vmem_limit_bytes=16 * MIB),
        cost_estimate=pl.CostEstimate(flops=10**7, bytes_accessed=5 * 10**6, transcendentals=0),
        name="covariance_columns",
    )(mp_index, own, near, far, row_scale, col_scale)


def whiten_kernel(
    total_rows, place_ref, own_ref, near_ref, far_ref, rs_ref, cs_ref, wide_ref, u_ref, row_ref, col_ref,
    old_hbm, low_hbm, proj_hbm, head_hbm, standard_hbm, normed_hbm,
    grad_ref, sums_ref, spill_ref,
    w, blk, t, wide, u, inv, white, old, low, proj, head, standard, normed, sems,
):
    n = w.shape[0]
    half = inv.shape[0]
    steps = n // WIDE
    mp = place_ref[0] % 2
    copies = [
        pltpu.make_async_copy(source, target, sems.at[i])
        for i, (source, target) in enumerate(
            (
                (old_hbm, old),
                (low_hbm, low),
                (proj_hbm, proj),
                (head_hbm, head),
                (standard_hbm, standard),
                (normed_hbm, normed),
            )
        )
    ]
    for copy in copies:
        copy.start()
    copies[0].wait()
    own, other = panel_source(own_ref, near_ref, far_ref)
    for index in range(2):
        @pl.when(mp == index)
        def _():
            load_panels(w, old, own, PANELS[index], (rs_ref, cs_ref), total_rows)
            load_panels(w, old, other, PANELS[1 - index], (rs_ref, cs_ref), total_rows)

    wide[...] = wide_ref[...]
    u[...] = u_ref[...]

    def step(k, carry):
        @pl.when((k > 0) | (mp == 0))
        def _():
            wide_factor(w, k, blk, t, wide)

        def whole_step(index):
            small = wide[...]
            if index > 0:
                eliminate(index, w, u, small)
            else:
                @pl.when(mp == 0)
                def _():
                    eliminate(index, w, u, small)

            @pl.when(mp == index * WIDE // half)
            def _():
                here = slice(index * WIDE % half, index * WIDE % half + WIDE)
                last = (index + 1) * WIDE
                inv[here, :last] = u[:, :last]
                if last < n:
                    inv[here, last:] = jnp.zeros((WIDE, n - last), F32)

            if index + 1 < steps:
                update_below(index, w, u, small)

        for index in range(steps):
            pl.when(k == index)(lambda index=index: whole_step(index))
        return carry

    lax.fori_loop(0, jnp.where(mp == 0, half // WIDE, steps), step, 0)
    for copy in copies[1:]:
        copy.wait()
    residual_kernel(
        total_rows, place_ref[0] < 2, inv, low, proj, row_ref, col_ref, head, standard, normed,
        grad_ref, sums_ref, spill_ref, white,
    )


def first_factor(mp_index, own, cov_old, row_scale, col_scale, total_rows):
    n = cov_old.shape[0]
    vmem = pl.BlockSpec(memory_space=pltpu.VMEM)

    def kernel(*refs):
        first_kernel(total_rows, *refs)

    return pl.pallas_call(
        kernel,
        out_shape=(
            jax.ShapeDtypeStruct((WIDE, WIDE), F32),
            jax.ShapeDtypeStruct((WIDE, n), F32),
        ),
        in_specs=[
            pl.BlockSpec(memory_space=pltpu.SMEM),
            vmem,
            pl.BlockSpec(memory_space=pl.ANY),
            vmem,
            vmem,
        ],
        out_specs=(vmem, vmem),
        scratch_shapes=[
            pltpu.VMEM((n, n), F32),
            pltpu.VMEM((BLOCK, BLOCK), F32),
            pltpu.VMEM((BLOCK, BLOCK), F32),
            pltpu.VMEM((n, WIDE), F32),
            pltpu.SemaphoreType.DMA,
        ],
        compiler_params=pltpu.CompilerParams(vmem_limit_bytes=20 * MIB),
        cost_estimate=pl.CostEstimate(flops=15 * 10**9, bytes_accessed=10**7, transcendentals=0),
        name="first_factor",
    )(mp_index, own, cov_old, row_scale, col_scale)


def residual_kernel(
    total_rows, is_image, inv_ref, low_ref, proj_ref, row_ref, col_ref, head_ref, standard_ref,
    normed_ref, grad_ref, sums_ref, spill_ref, white,
):
    rows, half = proj_ref.shape
    width = low_ref.shape[1]
    left = inv_ref[...]
    high = left.astype(BF16)
    left = left - high.astype(F32)
    middle = left.astype(BF16)
    small = (left - middle.astype(F32)).astype(BF16)
    dims = (((1,), (1,)), ((), ()))
    tile = 256
    for r in range(0, rows, tile):
        low = low_ref[r : r + tile, :]
        value = lax.dot_general(low, small, dims, preferred_element_type=F32)
        value += lax.dot_general(low, middle, dims, preferred_element_type=F32)
        value += lax.dot_general(low, high, dims, preferred_element_type=F32)
        white[r : r + tile, :] = value.astype(BF16)
    lane = lax.broadcasted_iota(jnp.int32, (tile, rows), 1)
    sub = lax.broadcasted_iota(jnp.int32, (tile, rows), 0)
    wanted = jnp.where(is_image, 1, 0)
    gain = jnp.zeros((1, width), F32)
    shift = jnp.zeros((1, width), F32)
    total = jnp.zeros((1, half), F32)
    for r in range(0, rows, tile):
        from_image = jnp.where(col_ref[r : r + tile, :] == lane, wanted, 0)
        from_text = jnp.where(row_ref[...] == sub + r, 1 - wanted, 0)
        chosen = (from_image + from_text).astype(F32).astype(BF16)
        targets = jnp.dot(chosen, white[...], preferred_element_type=F32)
        residual = proj_ref[r : r + tile, :] - targets
        total += jnp.sum(residual * residual, axis=0, keepdims=True)
        grad = (residual * (1.0 / width)).astype(BF16)
        grad_ref[r : r + tile, :] = grad
        dnormed = lax.dot_general(grad, head_ref[...], dims, preferred_element_type=F32)
        gain += jnp.sum(standard_ref[r : r + tile, :] * dnormed, axis=0, keepdims=True)
        shift += jnp.sum(dnormed, axis=0, keepdims=True)
    sums_ref[0:1, :] = gain
    sums_ref[1:2, :] = shift
    loss_value = jnp.sum(total, axis=1, keepdims=True) / (2.0 * total_rows * width)
    sums_ref[2:8, :] = jnp.broadcast_to(loss_value, (6, width))
    kept = width - spill_ref.shape[0]
    spill_ref[...] = contract_rows(normed_ref[:, kept:], grad_ref[...])


def whitened_residual(
    place, own, near, far, row_scale, col_scale, wide, upper, pairs,
    cov_old, low, projected, head, standard, normed, spilled, total_rows,
):
    rows, half = projected.shape
    n = cov_old.shape[0]
    vmem = pl.BlockSpec(memory_space=pltpu.VMEM)
    anywhere = pl.BlockSpec(memory_space=pl.ANY)

    def kernel(*refs):
        whiten_kernel(total_rows, *refs)

    return pl.pallas_call(
        kernel,
        out_shape=(
            jax.ShapeDtypeStruct((rows, half), BF16),
            jax.ShapeDtypeStruct((8, n), F32),
            jax.ShapeDtypeStruct((spilled, half), F32),
        ),
        in_specs=[pl.BlockSpec(memory_space=pltpu.SMEM)] + [vmem] * 9 + [anywhere] * 6,
        out_specs=(vmem, vmem, vmem),
        scratch_shapes=[
            pltpu.VMEM((n, n), F32),
            pltpu.VMEM((BLOCK, BLOCK), F32),
            pltpu.VMEM((BLOCK, BLOCK), F32),
            pltpu.VMEM((WIDE, WIDE), F32),
            pltpu.VMEM((WIDE, n), F32),
            pltpu.VMEM((half, n), F32),
            pltpu.VMEM((rows, half), BF16),
            pltpu.VMEM((n, n), F32),
            pltpu.VMEM((rows, n), BF16),
            pltpu.VMEM((rows, half), F32),
            pltpu.VMEM(head.shape, BF16),
            pltpu.VMEM(standard.shape, F32),
            pltpu.VMEM(normed.shape, BF16),
            pltpu.SemaphoreType.DMA((6,)),
        ],
        compiler_params=pltpu.CompilerParams(vmem_limit_bytes=48 * MIB),
        cost_estimate=pl.CostEstimate(flops=60 * 10**9, bytes_accessed=2 * 10**7, transcendentals=0),
        name="whitened_residual",
    )(
        place, own, near, far, row_scale, col_scale, wide, upper, pairs[None, :], pairs[:, None],
        cov_old, low, projected, head, standard, normed,
    )


CHUNK_EXPONENT, NORM_EXPONENT, LOSS_EXPONENTS, LOSS_CODES = 384, 385, 386, 388


def exponent_of(value):
    return jnp.ceil(jnp.log2(jnp.maximum(jnp.abs(value), 1e-30)))


def codes_of(value, exponent):
    return jnp.clip(jnp.round(value * jnp.exp2(15.0 - exponent)), -32767.0, 32767.0)


def payload_kernel(
    text_width, place_ref, weight_ref, spill_ref, mine_ref, mp_ref, tower_ref, both_ref,
    out_ref, part, image, text, first, second,
):
    chunks, height, half = out_ref.shape
    spilled = spill_ref.shape[0]
    kept = weight_ref.shape[0] - spilled
    share = kept // chunks
    width = mine_ref.shape[1]
    place = place_ref[0]
    mine = mine_ref[...] + mp_ref[...]
    theirs = tower_ref[...] + both_ref[...]

    @pl.when(place < 2)
    def _():
        part[:kept, :] = weight_ref[:kept, :]
        image[...] = mine
        text[...] = theirs

    @pl.when(place >= 2)
    def _():
        part[:spilled, :] = spill_ref[...]
        part[spilled:kept, :] = weight_ref[: kept - spilled, :]
        image[...] = theirs
        text[...] = mine

    part[kept:, :] = jnp.zeros((part.shape[0] - kept, half), F32)
    second[...] = jnp.zeros(second.shape, F32)
    quarter = (width + text_width) // 2
    for index in range(4):
        @pl.when(place == index)
        def _():
            row = slice(index // 2, index // 2 + 1)
            pieces = [(image, c) for c in range(0, width, BLOCK)]
            pieces += [(text, c) for c in range(0, text_width, BLOCK)]
            start = (index % 2) * quarter // BLOCK
            for i, (ref, c) in enumerate(pieces[start : start + quarter // BLOCK]):
                if i * BLOCK < half:
                    first[:, i * BLOCK : (i + 1) * BLOCK] = ref[row, c : c + BLOCK]
                else:
                    at = i * BLOCK - half
                    second[:, at : at + BLOCK] = ref[row, c : c + BLOCK]

    lane = lax.broadcasted_iota(jnp.int32, (1, half), 1)
    top = jnp.maximum(
        jnp.max(jnp.abs(first[...]), axis=1, keepdims=True),
        jnp.max(jnp.abs(second[...]), axis=1, keepdims=True),
    )
    norm_exponent = exponent_of(top)
    loss = jnp.where(lane % 2 == 0, image[2:3, :half], text[2:3, :half])
    loss_exponent = exponent_of(loss)
    tail = jnp.where(lane < LOSS_CODES, loss_exponent, codes_of(loss, loss_exponent))
    tail = jnp.where(lane == NORM_EXPONENT, norm_exponent, tail)
    tail = jnp.where(lane < CHUNK_EXPONENT, codes_of(second[...], norm_exponent), tail)
    tail = jnp.where(lane < LOSS_CODES + 2, tail, 0.0)
    head_row = codes_of(first[...], norm_exponent)
    sub = lax.broadcasted_iota(jnp.int32, (height, half), 0)
    for c in range(chunks):
        value = part[c * share : c * share + height, :]
        bound = jnp.max(jnp.where(sub < share, jnp.abs(value), 0.0), axis=0, keepdims=True)
        exponent = exponent_of(jnp.max(bound, axis=1, keepdims=True))
        last = jnp.where(lane == CHUNK_EXPONENT, exponent, tail)
        codes = jnp.where(
            sub < share, codes_of(value, exponent), jnp.where(sub == share, head_row, last)
        )
        out_ref[c] = codes.astype(jnp.int32).astype(jnp.int16)


def gradient_payload(place, weight, spill, mine, by_mp, by_tower, by_both, chunks, text_width):
    width, half = weight.shape
    height = (width - spill.shape[0]) // chunks + 2
    vmem = pl.BlockSpec(memory_space=pltpu.VMEM)

    def kernel(*refs):
        payload_kernel(text_width, *refs)

    return pl.pallas_call(
        kernel,
        out_shape=jax.ShapeDtypeStruct((chunks, height, half), jnp.int16),
        in_specs=[pl.BlockSpec(memory_space=pltpu.SMEM)] + [vmem] * 6,
        out_specs=vmem,
        scratch_shapes=[
            pltpu.VMEM((width - spill.shape[0] + 8, half), F32),
            pltpu.VMEM((8, width), F32),
            pltpu.VMEM((8, width), F32),
            pltpu.VMEM((1, half), F32),
            pltpu.VMEM((1, half), F32),
        ],
        compiler_params=pltpu.CompilerParams(vmem_limit_bytes=20 * MIB),
        cost_estimate=pl.CostEstimate(flops=10**7, bytes_accessed=4 * 10**6, transcendentals=0),
        name="gradient_payload",
    )(place, weight, spill, mine, by_mp, by_tower, by_both)


def collect_kernel(got_ref, weight_ref, rest_ref):
    chunks, height, half = got_ref.shape
    sub = lax.broadcasted_iota(jnp.int32, (height, half), 0)
    lane = lax.broadcasted_iota(jnp.int32, (height, half), 1)
    total = jnp.zeros((height, half), F32)
    for c in range(chunks):
        value = got_ref[c].astype(jnp.int32).astype(F32)
        steps = jnp.exp2(value[height - 1 : height, CHUNK_EXPONENT : CHUNK_EXPONENT + BLOCK] - 15.0)

        def step(at):
            return steps[:, at - CHUNK_EXPONENT : at - CHUNK_EXPONENT + 1]

        loss_step = jnp.where(lane == LOSS_CODES, step(LOSS_EXPONENTS), step(LOSS_EXPONENTS + 1))
        last = jnp.where(lane < CHUNK_EXPONENT, step(NORM_EXPONENT), loss_step)
        total += value * jnp.where(
            sub < height - 2,
            step(CHUNK_EXPONENT),
            jnp.where(sub == height - 2, step(NORM_EXPONENT), last),
        )
    weight_ref[...] = total[: height - 2, :]
    rest_ref[...] = total[height - 8 :, :]


def collect(got):
    chunks, height, half = got.shape
    vmem = pl.BlockSpec(memory_space=pltpu.VMEM)
    return pl.pallas_call(
        collect_kernel,
        out_shape=(
            jax.ShapeDtypeStruct((height - 2, half), F32),
            jax.ShapeDtypeStruct((8, half), F32),
        ),
        in_specs=[vmem],
        out_specs=(vmem, vmem),
        compiler_params=pltpu.CompilerParams(vmem_limit_bytes=12 * MIB),
        cost_estimate=pl.CostEstimate(flops=10**7, bytes_accessed=10**6, transcendentals=0),
        name="collect",
    )(got)


def combine_kernel(share, encode, got_ref, out_ref):
    sources, pieces, height, _ = got_ref.shape
    sub = lax.broadcasted_iota(jnp.int32, (height, BLOCK), 0)
    for piece in range(pieces):
        total = jnp.zeros((height, BLOCK), F32)
        for source in range(sources):
            value = got_ref[source, piece].astype(jnp.int32).astype(F32)
            total += value * jnp.exp2(value[share : share + 1, :] - 15.0)
        if encode:
            total = jnp.where(sub < share, total, 0.0)
            exponent = exponent_of(jnp.max(jnp.abs(total), axis=0, keepdims=True))
            codes = jnp.where(sub == share, exponent, codes_of(total, exponent))
            codes = codes.astype(jnp.int32).astype(jnp.int16)
            for copy in range(out_ref.shape[0]):
                out_ref[copy, piece] = codes
        else:
            for copy in range(out_ref.shape[0]):
                out_ref[copy, piece * share : (piece + 1) * share, :] = total[:share, :]


def combine(got, share, encode, copies):
    _, pieces, height, _ = got.shape
    vmem = pl.BlockSpec(memory_space=pltpu.VMEM)

    def kernel(*refs):
        combine_kernel(share, encode, *refs)

    if encode:
        shape = jax.ShapeDtypeStruct((copies, pieces, height, BLOCK), jnp.int16)
    else:
        shape = jax.ShapeDtypeStruct((copies, pieces * share, BLOCK), F32)
    return pl.pallas_call(
        kernel,
        out_shape=shape,
        in_specs=[vmem],
        out_specs=vmem,
        compiler_params=pltpu.CompilerParams(vmem_limit_bytes=12 * MIB),
        cost_estimate=pl.CostEstimate(flops=10**6, bytes_accessed=2 * 10**6, transcendentals=0),
        name="combine",
    )(got)


def sum_panels(codes, share):
    dp_count, height, _ = codes.shape
    along = min(8, dp_count)
    across = dp_count // along
    z_groups = [[a * along + z for z in range(along)] for a in range(across)]
    yx_groups = [[a * along + z for a in range(across)] for z in range(along)]

    def exchange(value, groups):
        if value.shape[0] == 1:
            return value
        return lax.all_to_all(value, "dp", 0, 0, tiled=True, axis_index_groups=groups)

    got = exchange(codes.reshape(across, along, height, BLOCK), yx_groups)
    got = exchange(combine(got, share, True, along), z_groups)
    got = exchange(combine(got, share, False, across), yx_groups)
    return got.reshape(dp_count * share, BLOCK)


def body(
    image_feats,
    text_feats,
    image_gain,
    image_bias,
    text_gain,
    text_bias,
    image_head,
    text_head,
    running_cov,
    pair_index,
):
    is_image = lax.axis_index("tower") == 0
    mp_index = lax.axis_index("mp")
    rows, image_width = image_feats.shape
    text_width = text_feats.shape[1]
    half = image_head.shape[1]
    width = running_cov.shape[1]
    dp_count = lax.axis_size("dp")
    total_rows = rows * dp_count

    depth = image_width // 2
    text_head_padded = pad_rows(text_head, image_width)
    near, far = swap_halves(
        jnp.where(is_image, text_head[:depth], image_head[:depth]),
        jnp.where(is_image, text_head_padded[depth:], image_head[depth:]),
    )
    cov_old = flip(running_cov[0], "tower")

    def text_rows(feats):
        standard, normed = normalize(feats, text_gain, text_bias)
        return pad_cols(standard, image_width), pad_cols(normed, image_width)

    normed_far = lax.cond(
        is_image,
        lambda: text_rows(text_feats)[1],
        lambda: normalize(image_feats, image_gain, image_bias)[1],
    )
    head_far = jnp.where(is_image, text_head_padded, image_head)

    gain_far = jnp.where(is_image, jnp.pad(text_gain, (0, image_width - text_width)), image_gain)
    bias_far = jnp.where(is_image, jnp.pad(text_bias, (0, image_width - text_width)), image_bias)
    head_wide = head_far.astype(F32)
    spread = jnp.sum((gain_far[:, None] * head_wide) ** 2, axis=0)
    middle = jnp.sum(bias_far[:, None] * head_wide, axis=0)
    size = jnp.maximum(spread + middle * middle, 1e-30)
    scale_own = jnp.exp2(-jnp.clip(jnp.round(0.5 * jnp.log2(size)), -20.0, 20.0))
    scale_other = flip(scale_own, "mp")
    scales = jnp.where(
        mp_index == 0,
        jnp.concatenate([scale_own, scale_other]),
        jnp.concatenate([scale_other, scale_own]),
    )
    own_low = jnp.dot(normed_far, head_far, preferred_element_type=F32).astype(BF16)
    own_low = (own_low.astype(F32) * scale_own[None, :]).astype(BF16)
    mp_scalar = mp_index[None].astype(jnp.int32)
    low_far, cov_codes = covariance_part(
        mp_scalar, normed_far, own_low, near, far, scale_other[None, :], dp_count
    )
    cov_codes, image_later, text_later = lax.optimization_barrier(
        (cov_codes, image_feats, text_feats)
    )
    standard, normed = lax.cond(
        is_image,
        lambda: normalize(image_later, image_gain, image_bias),
        lambda: text_rows(text_later),
    )
    head_own = jnp.where(is_image, image_head, text_head_padded)
    projected = jnp.dot(normed, head_own, preferred_element_type=F32)
    share = PANEL_ROWS // dp_count
    gathered = sum_panels(cov_codes, share)
    near_panels, far_panels = swap_halves(
        gathered[: PANEL_ROWS // 2], gathered[PANEL_ROWS // 2 :]
    )
    row_scale, col_scale = scales[:, None], scales[None, :]
    wide, upper = first_factor(mp_scalar, gathered, cov_old, row_scale, col_scale, total_rows)
    near_panels, far_panels, wide, upper = lax.optimization_barrier(
        (near_panels, far_panels, wide, upper)
    )
    per_tower = (image_width + text_width) // 2
    place = lax.axis_index("tower") * 2 + mp_index
    place_scalar = place[None].astype(jnp.int32)
    grad_low, sums, spill = whitened_residual(
        place_scalar, gathered, near_panels, far_panels, row_scale, col_scale, wide, upper,
        pair_index % rows, cov_old, low_far, projected, head_own, standard, normed,
        image_width - per_tower, total_rows,
    )
    spill = flip(spill, "tower")
    across = [(i, 3 - i) for i in range(4)]
    sums_mp, sums_tower = flip(sums, "mp"), flip(sums, "tower")
    sums_both = lax.ppermute(sums, ("tower", "mp"), across)
    weight_grad = contract_rows(normed, grad_low)
    payload = gradient_payload(
        place_scalar, weight_grad, spill, sums, sums_mp, sums_tower, sums_both,
        dp_count, text_width,
    )
    payload, own_panels, near_panels, far_panels = lax.optimization_barrier(
        (payload, gathered, near_panels, far_panels)
    )
    got = lax.all_to_all(payload, "dp", 0, 0, tiled=True)
    cov_cols = covariance_columns(
        mp_scalar, own_panels, near_panels, far_panels, row_scale, col_scale, total_rows
    )
    new_cov = flip(cov_cols, "tower") + 0.5 * lax.dynamic_slice_in_dim(
        running_cov[0], mp_index * half, half, 1
    )
    got, new_cov = lax.optimization_barrier((got, new_cov))
    head_grads, rest = collect(got)
    rest_mp, rest_tower = flip(rest, "mp"), flip(rest, "tower")
    rest_both = lax.ppermute(rest, ("tower", "mp"), across)
    parts = [rest, rest_mp, rest_tower, rest_both]
    quarters = []
    for index in range(4):
        chosen = parts[0]
        for other in range(1, 4):
            chosen = jnp.where(place == index ^ other, parts[other], chosen)
        quarters.append(chosen)
    flat = jnp.concatenate(
        [v for q in quarters for v in (q[6], q[7, : per_tower - half])]
    )
    norm_grads = flat.reshape(2, image_width + text_width)
    losses = rest[7, LOSS_CODES : LOSS_CODES + 2]
    return new_cov[None], head_grads, norm_grads, losses


def solution(mesh):
    return jax.shard_map(
        body,
        mesh=mesh,
        in_specs=(
            P("dp", None),
            P("dp", None),
            P(),
            P(),
            P(),
            P(),
            P(None, "mp"),
            P(None, "mp"),
            P("tower", None, None),
            P("dp"),
        ),
        out_specs=(P("tower", None, "mp"), P(("tower", "dp"), "mp"), P(), P()),
        check_vma=False,
    )
```

```python
import jax
import jax.numpy as jnp
from jax import lax
from jax.experimental import pallas as pl
from jax.experimental.pallas import tpu as pltpu
from jax.sharding import PartitionSpec as P

EPSILON = 1e-05
F32 = jnp.float32
BF16 = jnp.bfloat16
BLOCK = 128
GROUP = 8
PANELS = {
    1: ((0, 0, 8), (1, 1, 7), (2, 2, 3)),
    0: ((2, 5, 3), (3, 3, 5), (4, 4, 4), (5, 5, 3), (6, 6, 2), (7, 7, 1)),
}
PRODUCTS = {
    1: (((0, 2), 0, (0, 1)), ((2, 3), 2, (2,))),
    0: (((2, 4), 3, (0, 1)), ((4, 6), 4, (2, 3)), ((6, 8), 6, (4, 5))),
}
PANEL_ROWS = 18 * BLOCK
WIDE = 2 * BLOCK
MIB = 1024 * 1024


def flip(value, axis):
    return lax.ppermute(value, axis, [(0, 1), (1, 0)])


def swap_halves(first, second):
    dp_count = lax.axis_size("dp")
    x_hi_bit = 8 if dp_count == 64 else 1
    pairs = []
    for dp in range(dp_count):
        for mp in range(2):
            x_hi = (dp // x_hi_bit) % 2
            x = (x_hi * 2 + mp + (-1 if mp == 0 else 1)) % 4
            other = dp - x_hi * x_hi_bit + (x // 2) * x_hi_bit
            pairs.append((dp * 2 + mp, other * 2 + x % 2))
    return flip(first, "mp"), lax.ppermute(second, ("dp", "mp"), pairs)


def normalize(features, gain, bias):
    values = features.astype(F32)
    mean = jnp.mean(values, axis=1, keepdims=True)
    centered = values - mean
    var = jnp.mean(centered * centered, axis=1, keepdims=True)
    standard = centered * lax.rsqrt(var + EPSILON)
    return standard, (standard * gain[None, :] + bias[None, :]).astype(BF16)


def pad_cols(value, width):
    return jnp.pad(value, ((0, 0), (0, width - value.shape[1])))


def pad_rows(value, height):
    return jnp.pad(value, ((0, height - value.shape[0]), (0, 0)))


def contract_rows(a, b):
    return lax.dot_general(a, b, (((0,), (0,)), ((), ())), preferred_element_type=F32)


def precise_dot(a, b, dims):
    return lax.dot_general(
        a, b, (dims, ((), ())), precision=lax.Precision.HIGHEST, preferred_element_type=F32
    )


def tree_sum(terms):
    terms = list(terms)
    while len(terms) > 1:
        terms = [
            terms[a] + terms[a + 1] if a + 1 < len(terms) else terms[a]
            for a in range(0, len(terms), 2)
        ]
    return terms[0]


def factor_block(w_ref, t_ref):
    n = w_ref.shape[0]
    sub = lax.broadcasted_iota(jnp.int32, (GROUP, n), 0)
    lane = lax.broadcasted_iota(jnp.int32, (GROUP, n), 1)
    rows = [w_ref[GROUP * i : GROUP * (i + 1), :] for i in range(n // GROUP)]

    def spread(value):
        return jnp.broadcast_to(value, (GROUP, n))

    for g in range(n // GROUP):
        first = GROUP * g
        inside = (lane >= first) & (lane < first + GROUP)
        cols = [spread(rows[g][:, first + j : first + j + 1]) for j in range(GROUP)]
        e = [[spread(cols[j][i : i + 1, :]) for j in range(i + 1)] for i in range(GROUP)]
        full = jnp.where(inside, jnp.where(lane - first == sub, 1.0, 0.0), rows[g])
        right = [spread(full[k : k + 1, :]) for k in range(GROUP)]
        low = [[None] * GROUP for _ in range(GROUP)]
        roots, upper = [], []
        for j in range(GROUP):
            root = lax.rsqrt(e[j][j])
            roots.append(root)
            upper.append(right[j] * root)
            for i in range(j + 1, GROUP):
                low[i][j] = e[i][j] * root
            for k in range(j + 1, GROUP):
                right[k] = right[k] - low[k][j] * upper[j]
                for i in range(k, GROUP):
                    e[i][k] = e[i][k] - low[i][j] * low[k][j]
        result = upper[-1]
        for j in range(GROUP - 1):
            result = jnp.where(sub == j, upper[j], result)
        t_ref[first : first + GROUP, :] = jnp.where(lane < first + GROUP, result, 0.0)
        for i in range(g + 1, n // GROUP):
            left = []
            for j in range(GROUP):
                entry = spread(rows[i][:, first + j : first + j + 1])
                for k in range(j):
                    entry = entry - left[k] * low[j][k]
                left.append(entry * roots[j])
            rows[i] = jnp.where(inside, 0.0, rows[i]) - tree_sum(
                left[k] * upper[k] for k in range(GROUP)
            )


def covariance_kernel(mp_ref, normed_ref, own_ref, near_ref, far_ref, scale_ref, low_ref, out_ref, panel):
    depth, half = near_ref.shape
    other = jnp.dot(normed_ref[:, :depth], near_ref[...], preferred_element_type=F32)
    other += jnp.dot(normed_ref[:, depth:], far_ref[...], preferred_element_type=F32)
    other = (other.astype(BF16).astype(F32) * scale_ref[...]).astype(BF16)

    def products(index):
        low_ref[:, index * half : (index + 1) * half] = own_ref[...]
        low_ref[:, (1 - index) * half : (2 - index) * half] = other
        offsets = [0]
        for _, _, count in PANELS[index]:
            offsets.append(offsets[-1] + count * BLOCK)
        for (first, last), top, members in PRODUCTS[index]:
            bottom = max(PANELS[index][p][1] + PANELS[index][p][2] for p in members)
            product = contract_rows(
                low_ref[:, top * BLOCK : bottom * BLOCK], low_ref[:, first * BLOCK : last * BLOCK]
            )
            for p in members:
                col, row, count = PANELS[index][p]
                panel[offsets[p] : offsets[p + 1], :] = product[
                    (row - top) * BLOCK : (row - top + count) * BLOCK,
                    (col - first) * BLOCK : (col - first + 1) * BLOCK,
                ]

    for index in range(2):
        pl.when(mp_ref[0] == index)(lambda index=index: products(index))
    chunks, height, _ = out_ref.shape
    share = PANEL_ROWS // chunks
    panel[PANEL_ROWS:, :] = jnp.zeros((panel.shape[0] - PANEL_ROWS, BLOCK), F32)
    sub = lax.broadcasted_iota(jnp.int32, (height, BLOCK), 0)
    for c in range(chunks):
        value = panel[c * share : c * share + height, :]
        top = jnp.max(jnp.where(sub < share, jnp.abs(value), 0.0), axis=0, keepdims=True)
        exponent = jnp.ceil(jnp.log2(jnp.maximum(top, 1e-30)))
        codes = jnp.clip(jnp.round(value * jnp.exp2(15.0 - exponent)), -32767.0, 32767.0)
        codes = jnp.where(sub < share, codes, jnp.where(sub == share, exponent, 0.0))
        out_ref[c] = codes.astype(jnp.int32).astype(jnp.int16)


def covariance_part(mp_index, normed, own, near, far, scale, chunks):
    rows, half = own.shape
    share = PANEL_ROWS // chunks
    height = share + 8 - share % 8
    vmem = pl.BlockSpec(memory_space=pltpu.VMEM)
    return pl.pallas_call(
        covariance_kernel,
        out_shape=(
            jax.ShapeDtypeStruct((rows, 2 * half), BF16),
            jax.ShapeDtypeStruct((chunks, height, BLOCK), jnp.int16),
        ),
        in_specs=[pl.BlockSpec(memory_space=pltpu.SMEM)] + [vmem] * 5,
        out_specs=(vmem, vmem),
        scratch_shapes=[pltpu.VMEM((PANEL_ROWS + 8, BLOCK), F32)],
        compiler_params=pltpu.CompilerParams(vmem_limit_bytes=24 * MIB),
        cost_estimate=pl.CostEstimate(flops=3 * 10**9, bytes_accessed=10**7, transcendentals=0),
        name="covariance_part",
    )(mp_index, normed, own, near, far, scale)


def wide_factor(w_ref, k, blk, t, wide):
    a = pl.ds(pl.multiple_of(k * WIDE, WIDE), BLOCK)
    b = pl.ds(pl.multiple_of(k * WIDE + BLOCK, BLOCK), BLOCK)
    corner = w_ref[b, a]

    def half_step(h, carry):
        @pl.when(h == 0)
        def _():
            blk[...] = w_ref[a, a]

        @pl.when(h == 1)
        def _():
            first = t[...]
            wide[:BLOCK, :BLOCK] = first
            wide[:BLOCK, BLOCK:] = jnp.zeros((BLOCK, BLOCK), F32)
            left = precise_dot(corner, first, ((1,), (1,)))
            wide[BLOCK:, :BLOCK] = precise_dot(left, first, ((1,), (0,)))
            blk[...] = w_ref[b, b] - precise_dot(left, left, ((1,), (1,)))

        factor_block(blk, t)
        return carry

    lax.fori_loop(0, 2, half_step, 0)
    second = t[...]
    wide[BLOCK:, BLOCK:] = second
    wide[BLOCK:, :BLOCK] = -precise_dot(second, wide[BLOCK:, :BLOCK], ((1,), (0,)))


def load_panels(w, old_ref, source, panels, scales, total_rows):
    row_scale, col_scale = scales
    offset = 0
    for col, row, count in panels:
        there = slice(col * BLOCK, (col + 1) * BLOCK)
        for i in range(row, row + count):
            here = slice(i * BLOCK, (i + 1) * BLOCK)
            both = row_scale[here, :] * col_scale[:, there]
            value = 0.5 * old_ref[here, there] * both
            value += (0.5 / total_rows) * source(offset)
            w[here, there] = value
            if i > col:
                w[there, here] = value.T
            offset += BLOCK


def eliminate(k, w, u, small):
    first, last = k * WIDE, (k + 1) * WIDE
    n = w.shape[1]
    if first > 0:
        u[:, :first] = precise_dot(small, w[first:last, :first], ((1,), (0,)))
    u[:, first:last] = small
    if last < n:
        u[:, last:] = precise_dot(small, w[first:last, last:], ((1,), (0,)))


def update_below(k, w, u, small):
    first, last = k * WIDE, (k + 1) * WIDE
    left = precise_dot(w[last:, first:last], small, ((1,), (1,)))
    w[last:, first:last] = jnp.zeros((w.shape[0] - last, WIDE), F32)
    w[last:, :] -= precise_dot(left, u[...], ((1,), (0,)))


def first_kernel(
    total_rows, mp_ref, own_ref, old_hbm, rs_ref, cs_ref, wide_ref, u_ref, w, blk, t, old, sem
):
    @pl.when(mp_ref[0] == 1)
    def _():
        copy = pltpu.make_async_copy(old_hbm.at[:, pl.ds(0, WIDE)], old, sem)
        copy.start()
        copy.wait()

        def own(offset):
            return own_ref[offset : offset + BLOCK, :]

        load_panels(w, old, own, PANELS[1][:2], (rs_ref, cs_ref), total_rows)
        wide_factor(w, 0, blk, t, wide_ref)
        eliminate(0, w, u_ref, wide_ref[...])

    @pl.when(mp_ref[0] == 0)
    def _():
        wide_ref[...] = jnp.zeros(wide_ref.shape, F32)
        u_ref[...] = jnp.zeros(u_ref.shape, F32)


def panel_source(own_ref, near_ref, far_ref):
    split = near_ref.shape[0]

    def own(offset):
        return own_ref[offset : offset + BLOCK, :]

    def other(offset):
        if offset < split:
            return near_ref[offset : offset + BLOCK, :]
        return far_ref[offset - split : offset - split + BLOCK, :]

    return own, other


def columns_kernel(total_rows, mp_ref, own_ref, near_ref, far_ref, rs_ref, cs_ref, cov_ref, rows, cols):
    half = cov_ref.shape[1]
    own, other = panel_source(own_ref, near_ref, far_ref)
    rows[...] = 1.0 / rs_ref[...]
    cols[...] = (0.5 / total_rows) / cs_ref[...]

    def fill(index):
        for source, panels in ((own, PANELS[index]), (other, PANELS[1 - index])):
            offset = 0
            for col, row, count in panels:
                for i in range(row, row + count):
                    value = source(offset)
                    offset += BLOCK
                    for r, c in ((i, col),) if i == col else ((i, col), (col, i)):
                        if c * BLOCK // half != index:
                            continue
                        block = value if r == i else value.T
                        here = slice(r * BLOCK, (r + 1) * BLOCK)
                        there = slice(c * BLOCK, (c + 1) * BLOCK)
                        at = slice(c * BLOCK - index * half, (c + 1) * BLOCK - index * half)
                        cov_ref[here, at] = block * rows[here, :] * cols[:, there]

    for index in range(2):
        pl.when(mp_ref[0] == index)(lambda index=index: fill(index))


def covariance_columns(mp_index, own, near, far, row_scale, col_scale, total_rows):
    n = row_scale.shape[0]
    vmem = pl.BlockSpec(memory_space=pltpu.VMEM)

    def kernel(*refs):
        columns_kernel(total_rows, *refs)

    return pl.pallas_call(
        kernel,
        out_shape=jax.ShapeDtypeStruct((n, n // 2), F32),
        in_specs=[pl.BlockSpec(memory_space=pltpu.SMEM)] + [vmem] * 5,
        out_specs=vmem,
        scratch_shapes=[pltpu.VMEM((n, 1), F32), pltpu.VMEM((1, n), F32)],
        compiler_params=pltpu.CompilerParams(vmem_limit_bytes=16 * MIB),
        cost_estimate=pl.CostEstimate(flops=10**7, bytes_accessed=5 * 10**6, transcendentals=0),
        name="covariance_columns",
    )(mp_index, own, near, far, row_scale, col_scale)


def whiten_kernel(
    total_rows, place_ref, own_ref, near_ref, far_ref, rs_ref, cs_ref, wide_ref, u_ref, row_ref, col_ref,
    old_hbm, low_hbm, proj_hbm, head_hbm, standard_hbm, normed_hbm,
    grad_ref, sums_ref, spill_ref,
    w, blk, t, wide, u, inv, white, old, low, proj, head, standard, normed, sems,
):
    n = w.shape[0]
    half = inv.shape[0]
    steps = n // WIDE
    mp = place_ref[0] % 2
    copies = [
        pltpu.make_async_copy(source, target, sems.at[i])
        for i, (source, target) in enumerate(
            (
                (old_hbm, old),
                (low_hbm, low),
                (proj_hbm, proj),
                (head_hbm, head),
                (standard_hbm, standard),
                (normed_hbm, normed),
            )
        )
    ]
    for copy in copies:
        copy.start()
    copies[0].wait()
    own, other = panel_source(own_ref, near_ref, far_ref)
    for index in range(2):
        @pl.when(mp == index)
        def _():
            load_panels(w, old, own, PANELS[index], (rs_ref, cs_ref), total_rows)
            load_panels(w, old, other, PANELS[1 - index], (rs_ref, cs_ref), total_rows)

    wide[...] = wide_ref[...]
    u[...] = u_ref[...]

    def step(k, carry):
        @pl.when((k > 0) | (mp == 0))
        def _():
            wide_factor(w, k, blk, t, wide)

        def whole_step(index):
            small = wide[...]
            if index > 0:
                eliminate(index, w, u, small)
            else:
                @pl.when(mp == 0)
                def _():
                    eliminate(index, w, u, small)

            @pl.when(mp == index * WIDE // half)
            def _():
                here = slice(index * WIDE % half, index * WIDE % half + WIDE)
                last = (index + 1) * WIDE
                inv[here, :last] = u[:, :last]
                if last < n:
                    inv[here, last:] = jnp.zeros((WIDE, n - last), F32)

            if index + 1 < steps:
                update_below(index, w, u, small)

        for index in range(steps):
            pl.when(k == index)(lambda index=index: whole_step(index))
        return carry

    lax.fori_loop(0, jnp.where(mp == 0, half // WIDE, steps), step, 0)
    for copy in copies[1:]:
        copy.wait()
    residual_kernel(
        total_rows, place_ref[0] < 2, inv, low, proj, row_ref, col_ref, head, standard, normed,
        grad_ref, sums_ref, spill_ref, white,
    )


def first_factor(mp_index, own, cov_old, row_scale, col_scale, total_rows):
    n = cov_old.shape[0]
    vmem = pl.BlockSpec(memory_space=pltpu.VMEM)

    def kernel(*refs):
        first_kernel(total_rows, *refs)

    return pl.pallas_call(
        kernel,
        out_shape=(
            jax.ShapeDtypeStruct((WIDE, WIDE), F32),
            jax.ShapeDtypeStruct((WIDE, n), F32),
        ),
        in_specs=[
            pl.BlockSpec(memory_space=pltpu.SMEM),
            vmem,
            pl.BlockSpec(memory_space=pl.ANY),
            vmem,
            vmem,
        ],
        out_specs=(vmem, vmem),
        scratch_shapes=[
            pltpu.VMEM((n, n), F32),
            pltpu.VMEM((BLOCK, BLOCK), F32),
            pltpu.VMEM((BLOCK, BLOCK), F32),
            pltpu.VMEM((n, WIDE), F32),
            pltpu.SemaphoreType.DMA,
        ],
        compiler_params=pltpu.CompilerParams(vmem_limit_bytes=20 * MIB),
        cost_estimate=pl.CostEstimate(flops=15 * 10**9, bytes_accessed=10**7, transcendentals=0),
        name="first_factor",
    )(mp_index, own, cov_old, row_scale, col_scale)


def residual_kernel(
    total_rows, is_image, inv_ref, low_ref, proj_ref, row_ref, col_ref, head_ref, standard_ref,
    normed_ref, grad_ref, sums_ref, spill_ref, white,
):
    rows, half = proj_ref.shape
    width = low_ref.shape[1]
    left = inv_ref[...]
    high = left.astype(BF16)
    left = left - high.astype(F32)
    middle = left.astype(BF16)
    small = (left - middle.astype(F32)).astype(BF16)
    dims = (((1,), (1,)), ((), ()))
    tile = 256
    for r in range(0, rows, tile):
        low = low_ref[r : r + tile, :]
        value = lax.dot_general(low, small, dims, preferred_element_type=F32)
        value += lax.dot_general(low, middle, dims, preferred_element_type=F32)
        value += lax.dot_general(low, high, dims, preferred_element_type=F32)
        white[r : r + tile, :] = value.astype(BF16)
    lane = lax.broadcasted_iota(jnp.int32, (tile, rows), 1)
    sub = lax.broadcasted_iota(jnp.int32, (tile, rows), 0)
    wanted = jnp.where(is_image, 1, 0)
    gain = jnp.zeros((1, width), F32)
    shift = jnp.zeros((1, width), F32)
    total = jnp.zeros((1, half), F32)
    for r in range(0, rows, tile):
        from_image = jnp.where(col_ref[r : r + tile, :] == lane, wanted, 0)
        from_text = jnp.where(row_ref[...] == sub + r, 1 - wanted, 0)
        chosen = (from_image + from_text).astype(F32).astype(BF16)
        targets = jnp.dot(chosen, white[...], preferred_element_type=F32)
        residual = proj_ref[r : r + tile, :] - targets
        total += jnp.sum(residual * residual, axis=0, keepdims=True)
        grad = (residual * (1.0 / width)).astype(BF16)
        grad_ref[r : r + tile, :] = grad
        dnormed = lax.dot_general(grad, head_ref[...], dims, preferred_element_type=F32)
        gain += jnp.sum(standard_ref[r : r + tile, :] * dnormed, axis=0, keepdims=True)
        shift += jnp.sum(dnormed, axis=0, keepdims=True)
    sums_ref[0:1, :] = gain
    sums_ref[1:2, :] = shift
    loss_value = jnp.sum(total, axis=1, keepdims=True) / (2.0 * total_rows * width)
    sums_ref[2:8, :] = jnp.broadcast_to(loss_value, (6, width))
    kept = width - spill_ref.shape[0]
    spill_ref[...] = contract_rows(normed_ref[:, kept:], grad_ref[...])


def whitened_residual(
    place, own, near, far, row_scale, col_scale, wide, upper, pairs,
    cov_old, low, projected, head, standard, normed, spilled, total_rows,
):
    rows, half = projected.shape
    n = cov_old.shape[0]
    vmem = pl.BlockSpec(memory_space=pltpu.VMEM)
    anywhere = pl.BlockSpec(memory_space=pl.ANY)

    def kernel(*refs):
        whiten_kernel(total_rows, *refs)

    return pl.pallas_call(
        kernel,
        out_shape=(
            jax.ShapeDtypeStruct((rows, half), BF16),
            jax.ShapeDtypeStruct((8, n), F32),
            jax.ShapeDtypeStruct((spilled, half), F32),
        ),
        in_specs=[pl.BlockSpec(memory_space=pltpu.SMEM)] + [vmem] * 9 + [anywhere] * 6,
        out_specs=(vmem, vmem, vmem),
        scratch_shapes=[
            pltpu.VMEM((n, n), F32),
            pltpu.VMEM((BLOCK, BLOCK), F32),
            pltpu.VMEM((BLOCK, BLOCK), F32),
            pltpu.VMEM((WIDE, WIDE), F32),
            pltpu.VMEM((WIDE, n), F32),
            pltpu.VMEM((half, n), F32),
            pltpu.VMEM((rows, half), BF16),
            pltpu.VMEM((n, n), F32),
            pltpu.VMEM((rows, n), BF16),
            pltpu.VMEM((rows, half), F32),
            pltpu.VMEM(head.shape, BF16),
            pltpu.VMEM(standard.shape, F32),
            pltpu.VMEM(normed.shape, BF16),
            pltpu.SemaphoreType.DMA((6,)),
        ],
        compiler_params=pltpu.CompilerParams(vmem_limit_bytes=48 * MIB),
        cost_estimate=pl.CostEstimate(flops=60 * 10**9, bytes_accessed=2 * 10**7, transcendentals=0),
        name="whitened_residual",
    )(
        place, own, near, far, row_scale, col_scale, wide, upper, pairs[None, :], pairs[:, None],
        cov_old, low, projected, head, standard, normed,
    )


CHUNK_EXPONENT, NORM_EXPONENT, LOSS_EXPONENTS, LOSS_CODES = 384, 385, 386, 388


def exponent_of(value):
    return jnp.ceil(jnp.log2(jnp.maximum(jnp.abs(value), 1e-30)))


def codes_of(value, exponent):
    return jnp.clip(jnp.round(value * jnp.exp2(15.0 - exponent)), -32767.0, 32767.0)


def payload_kernel(
    text_width, place_ref, weight_ref, spill_ref, mine_ref, mp_ref, tower_ref, both_ref,
    out_ref, part, image, text, first, second,
):
    chunks, height, half = out_ref.shape
    spilled = spill_ref.shape[0]
    kept = weight_ref.shape[0] - spilled
    share = kept // chunks
    width = mine_ref.shape[1]
    place = place_ref[0]
    mine = mine_ref[...] + mp_ref[...]
    theirs = tower_ref[...] + both_ref[...]

    @pl.when(place < 2)
    def _():
        part[:kept, :] = weight_ref[:kept, :]
        image[...] = mine
        text[...] = theirs

    @pl.when(place >= 2)
    def _():
        part[:spilled, :] = spill_ref[...]
        part[spilled:kept, :] = weight_ref[: kept - spilled, :]
        image[...] = theirs
        text[...] = mine

    part[kept:, :] = jnp.zeros((part.shape[0] - kept, half), F32)
    second[...] = jnp.zeros(second.shape, F32)
    quarter = (width + text_width) // 2
    for index in range(4):
        @pl.when(place == index)
        def _():
            row = slice(index // 2, index // 2 + 1)
            pieces = [(image, c) for c in range(0, width, BLOCK)]
            pieces += [(text, c) for c in range(0, text_width, BLOCK)]
            start = (index % 2) * quarter // BLOCK
            for i, (ref, c) in enumerate(pieces[start : start + quarter // BLOCK]):
                if i * BLOCK < half:
                    first[:, i * BLOCK : (i + 1) * BLOCK] = ref[row, c : c + BLOCK]
                else:
                    at = i * BLOCK - half
                    second[:, at : at + BLOCK] = ref[row, c : c + BLOCK]

    lane = lax.broadcasted_iota(jnp.int32, (1, half), 1)
    top = jnp.maximum(
        jnp.max(jnp.abs(first[...]), axis=1, keepdims=True),
        jnp.max(jnp.abs(second[...]), axis=1, keepdims=True),
    )
    norm_exponent = exponent_of(top)
    loss = jnp.where(lane % 2 == 0, image[2:3, :half], text[2:3, :half])
    loss_exponent = exponent_of(loss)
    tail = jnp.where(lane < LOSS_CODES, loss_exponent, codes_of(loss, loss_exponent))
    tail = jnp.where(lane == NORM_EXPONENT, norm_exponent, tail)
    tail = jnp.where(lane < CHUNK_EXPONENT, codes_of(second[...], norm_exponent), tail)
    tail = jnp.where(lane < LOSS_CODES + 2, tail, 0.0)
    head_row = codes_of(first[...], norm_exponent)
    sub = lax.broadcasted_iota(jnp.int32, (height, half), 0)
    for c in range(chunks):
        value = part[c * share : c * share + height, :]
        bound = jnp.max(jnp.where(sub < share, jnp.abs(value), 0.0), axis=0, keepdims=True)
        exponent = exponent_of(jnp.max(bound, axis=1, keepdims=True))
        last = jnp.where(lane == CHUNK_EXPONENT, exponent, tail)
        codes = jnp.where(
            sub < share, codes_of(value, exponent), jnp.where(sub == share, head_row, last)
        )
        out_ref[c] = codes.astype(jnp.int32).astype(jnp.int16)


def gradient_payload(place, weight, spill, mine, by_mp, by_tower, by_both, chunks, text_width):
    width, half = weight.shape
    height = (width - spill.shape[0]) // chunks + 2
    vmem = pl.BlockSpec(memory_space=pltpu.VMEM)

    def kernel(*refs):
        payload_kernel(text_width, *refs)

    return pl.pallas_call(
        kernel,
        out_shape=jax.ShapeDtypeStruct((chunks, height, half), jnp.int16),
        in_specs=[pl.BlockSpec(memory_space=pltpu.SMEM)] + [vmem] * 6,
        out_specs=vmem,
        scratch_shapes=[
            pltpu.VMEM((width - spill.shape[0] + 8, half), F32),
            pltpu.VMEM((8, width), F32),
            pltpu.VMEM((8, width), F32),
            pltpu.VMEM((1, half), F32),
            pltpu.VMEM((1, half), F32),
        ],
        compiler_params=pltpu.CompilerParams(vmem_limit_bytes=20 * MIB),
        cost_estimate=pl.CostEstimate(flops=10**7, bytes_accessed=4 * 10**6, transcendentals=0),
        name="gradient_payload",
    )(place, weight, spill, mine, by_mp, by_tower, by_both)


def collect_kernel(got_ref, weight_ref, rest_ref):
    chunks, height, half = got_ref.shape
    sub = lax.broadcasted_iota(jnp.int32, (height, half), 0)
    lane = lax.broadcasted_iota(jnp.int32, (height, half), 1)
    total = jnp.zeros((height, half), F32)
    for c in range(chunks):
        value = got_ref[c].astype(jnp.int32).astype(F32)
        steps = jnp.exp2(value[height - 1 : height, CHUNK_EXPONENT : CHUNK_EXPONENT + BLOCK] - 15.0)

        def step(at):
            return steps[:, at - CHUNK_EXPONENT : at - CHUNK_EXPONENT + 1]

        loss_step = jnp.where(lane == LOSS_CODES, step(LOSS_EXPONENTS), step(LOSS_EXPONENTS + 1))
        last = jnp.where(lane < CHUNK_EXPONENT, step(NORM_EXPONENT), loss_step)
        total += value * jnp.where(
            sub < height - 2,
            step(CHUNK_EXPONENT),
            jnp.where(sub == height - 2, step(NORM_EXPONENT), last),
        )
    weight_ref[...] = total[: height - 2, :]
    rest_ref[...] = total[height - 8 :, :]


def collect(got):
    chunks, height, half = got.shape
    vmem = pl.BlockSpec(memory_space=pltpu.VMEM)
    return pl.pallas_call(
        collect_kernel,
        out_shape=(
            jax.ShapeDtypeStruct((height - 2, half), F32),
            jax.ShapeDtypeStruct((8, half), F32),
        ),
        in_specs=[vmem],
        out_specs=(vmem, vmem),
        compiler_params=pltpu.CompilerParams(vmem_limit_bytes=12 * MIB),
        cost_estimate=pl.CostEstimate(flops=10**7, bytes_accessed=10**6, transcendentals=0),
        name="collect",
    )(got)


def combine_kernel(share, encode, got_ref, out_ref):
    sources, pieces, height, _ = got_ref.shape
    sub = lax.broadcasted_iota(jnp.int32, (height, BLOCK), 0)
    for piece in range(pieces):
        total = jnp.zeros((height, BLOCK), F32)
        for source in range(sources):
            value = got_ref[source, piece].astype(jnp.int32).astype(F32)
            total += value * jnp.exp2(value[share : share + 1, :] - 15.0)
        if encode:
            total = jnp.where(sub < share, total, 0.0)
            exponent = exponent_of(jnp.max(jnp.abs(total), axis=0, keepdims=True))
            codes = jnp.where(sub == share, exponent, codes_of(total, exponent))
            codes = codes.astype(jnp.int32).astype(jnp.int16)
            for copy in range(out_ref.shape[0]):
                out_ref[copy, piece] = codes
        else:
            for copy in range(out_ref.shape[0]):
                out_ref[copy, piece * share : (piece + 1) * share, :] = total[:share, :]


def combine(got, share, encode, copies):
    _, pieces, height, _ = got.shape
    vmem = pl.BlockSpec(memory_space=pltpu.VMEM)

    def kernel(*refs):
        combine_kernel(share, encode, *refs)

    if encode:
        shape = jax.ShapeDtypeStruct((copies, pieces, height, BLOCK), jnp.int16)
    else:
        shape = jax.ShapeDtypeStruct((copies, pieces * share, BLOCK), F32)
    return pl.pallas_call(
        kernel,
        out_shape=shape,
        in_specs=[vmem],
        out_specs=vmem,
        compiler_params=pltpu.CompilerParams(vmem_limit_bytes=12 * MIB),
        cost_estimate=pl.CostEstimate(flops=10**6, bytes_accessed=2 * 10**6, transcendentals=0),
        name="combine",
    )(got)


def sum_panels(codes, share):
    dp_count, height, _ = codes.shape
    along = min(8, dp_count)
    across = dp_count // along
    z_groups = [[a * along + z for z in range(along)] for a in range(across)]
    yx_groups = [[a * along + z for a in range(across)] for z in range(along)]

    def exchange(value, groups):
        if value.shape[0] == 1:
            return value
        return lax.all_to_all(value, "dp", 0, 0, tiled=True, axis_index_groups=groups)

    got = exchange(codes.reshape(across, along, height, BLOCK), yx_groups)
    got = exchange(combine(got, share, True, along), z_groups)
    got = exchange(combine(got, share, False, across), yx_groups)
    return got.reshape(dp_count * share, BLOCK)


def body(
    image_feats,
    text_feats,
    image_gain,
    image_bias,
    text_gain,
    text_bias,
    image_head,
    text_head,
    running_cov,
    pair_index,
):
    is_image = lax.axis_index("tower") == 0
    mp_index = lax.axis_index("mp")
    rows, image_width = image_feats.shape
    text_width = text_feats.shape[1]
    half = image_head.shape[1]
    width = running_cov.shape[1]
    dp_count = lax.axis_size("dp")
    total_rows = rows * dp_count

    depth = image_width // 2
    text_head_padded = pad_rows(text_head, image_width)
    near, far = swap_halves(
        jnp.where(is_image, text_head[:depth], image_head[:depth]),
        jnp.where(is_image, text_head_padded[depth:], image_head[depth:]),
    )
    cov_old = flip(running_cov[0], "tower")

    def text_rows(feats):
        standard, normed = normalize(feats, text_gain, text_bias)
        return pad_cols(standard, image_width), pad_cols(normed, image_width)

    normed_far = lax.cond(
        is_image,
        lambda: text_rows(text_feats)[1],
        lambda: normalize(image_feats, image_gain, image_bias)[1],
    )
    head_far = jnp.where(is_image, text_head_padded, image_head)

    gain_far = jnp.where(is_image, jnp.pad(text_gain, (0, image_width - text_width)), image_gain)
    bias_far = jnp.where(is_image, jnp.pad(text_bias, (0, image_width - text_width)), image_bias)
    head_wide = head_far.astype(F32)
    spread = jnp.sum((gain_far[:, None] * head_wide) ** 2, axis=0)
    middle = jnp.sum(bias_far[:, None] * head_wide, axis=0)
    size = jnp.maximum(spread + middle * middle, 1e-30)
    scale_own = jnp.exp2(-jnp.clip(jnp.round(0.5 * jnp.log2(size)), -20.0, 20.0))
    scale_other = flip(scale_own, "mp")
    scales = jnp.where(
        mp_index == 0,
        jnp.concatenate([scale_own, scale_other]),
        jnp.concatenate([scale_other, scale_own]),
    )
    own_low = jnp.dot(normed_far, head_far, preferred_element_type=F32).astype(BF16)
    own_low = (own_low.astype(F32) * scale_own[None, :]).astype(BF16)
    mp_scalar = mp_index[None].astype(jnp.int32)
    low_far, cov_codes = covariance_part(
        mp_scalar, normed_far, own_low, near, far, scale_other[None, :], dp_count
    )
    cov_codes, image_later, text_later = lax.optimization_barrier(
        (cov_codes, image_feats, text_feats)
    )
    standard, normed = lax.cond(
        is_image,
        lambda: normalize(image_later, image_gain, image_bias),
        lambda: text_rows(text_later),
    )
    head_own = jnp.where(is_image, image_head, text_head_padded)
    projected = jnp.dot(normed, head_own, preferred_element_type=F32)
    share = PANEL_ROWS // dp_count
    gathered = sum_panels(cov_codes, share)
    near_panels, far_panels = swap_halves(
        gathered[: PANEL_ROWS // 2], gathered[PANEL_ROWS // 2 :]
    )
    row_scale, col_scale = scales[:, None], scales[None, :]
    wide, upper = first_factor(mp_scalar, gathered, cov_old, row_scale, col_scale, total_rows)
    near_panels, far_panels, wide, upper = lax.optimization_barrier(
        (near_panels, far_panels, wide, upper)
    )
    per_tower = (image_width + text_width) // 2
    place = lax.axis_index("tower") * 2 + mp_index
    place_scalar = place[None].astype(jnp.int32)
    grad_low, sums, spill = whitened_residual(
        place_scalar, gathered, near_panels, far_panels, row_scale, col_scale, wide, upper,
        pair_index % rows, cov_old, low_far, projected, head_own, standard, normed,
        image_width - per_tower, total_rows,
    )
    spill = flip(spill, "tower")
    across = [(i, 3 - i) for i in range(4)]
    sums_mp, sums_tower = flip(sums, "mp"), flip(sums, "tower")
    sums_both = lax.ppermute(sums, ("tower", "mp"), across)
    weight_grad = contract_rows(normed, grad_low)
    payload = gradient_payload(
        place_scalar, weight_grad, spill, sums, sums_mp, sums_tower, sums_both,
        dp_count, text_width,
    )
    payload, own_panels, near_panels, far_panels = lax.optimization_barrier(
        (payload, gathered, near_panels, far_panels)
    )
    got = lax.all_to_all(payload, "dp", 0, 0, tiled=True)
    cov_cols = covariance_columns(
        mp_scalar, own_panels, near_panels, far_panels, row_scale, col_scale, total_rows
    )
    swapped = flip(cov_cols, "tower")
    head_grads, rest = collect(got)
    rest_mp, rest_tower = flip(rest, "mp"), flip(rest, "tower")
    rest_both = lax.ppermute(rest, ("tower", "mp"), across)
    new_cov = swapped + 0.5 * lax.dynamic_slice_in_dim(
        running_cov[0], mp_index * half, half, 1
    )
    rest_mp, rest_tower, rest_both, new_cov = lax.optimization_barrier(
        (rest_mp, rest_tower, rest_both, new_cov)
    )
    parts = [rest, rest_mp, rest_tower, rest_both]
    quarters = []
    for index in range(4):
        chosen = parts[0]
        for other in range(1, 4):
            chosen = jnp.where(place == index ^ other, parts[other], chosen)
        quarters.append(chosen)
    flat = jnp.concatenate(
        [v for q in quarters for v in (q[6], q[7, : per_tower - half])]
    )
    norm_grads = flat.reshape(2, image_width + text_width)
    losses = rest[7, LOSS_CODES : LOSS_CODES + 2]
    return new_cov[None], head_grads, norm_grads, losses


def solution(mesh):
    return jax.shard_map(
        body,
        mesh=mesh,
        in_specs=(
            P("dp", None),
            P("dp", None),
            P(),
            P(),
            P(),
            P(),
            P(None, "mp"),
            P(None, "mp"),
            P("tower", None, None),
            P("dp"),
        ),
        out_specs=(P("tower", None, "mp"), P(("tower", "dp"), "mp"), P(), P()),
        check_vma=False,
    )
```
